512 devices in a mesh: row: 16 (over y, core), col: 32 (over z, x).
Axes of the slice: x: 4, y: 8, z: 8, core: 2. Of those that a mesh axis runs over, the one named last changes fastest.
Arguments:
- matrix: float32 [4, 16, 256, 2, 32, 256], P(None, 'row', None, None, 'col'), may hold values from -1.1 to 65.1, as said below
- precision: int32 [4, 16, 2, 32], P(None, 'row', None, 'col'), may hold values from 0 to 2, as said below
- first_col: int32 [1], replicated, may hold values from 0 to 46
Outputs:
- factored: float32 [4, 16, 256, 2, 32, 256], P(None, 'row', None, None, 'col')
The draws below stay inside these ranges and needn't reach their ends.
Inputs may be any that keep to these rules, and one draw needn't show every extreme that they name: `precision`: 2 marks a float32 tile, 1 a bfloat16 tile, 0 a dropped tile. Every diagonal tile is 2 and every tile above the diagonal is 0; down each tile column from the diagonal the values never rise. `matrix`: diagonal tiles are symmetric and positive definite; tiles above the diagonal are not read.
All inputs are finite; a program needn't handle non-finite values.
Results may differ from the reference program's by a relative error of at most 0.0003.
Values sent between devices are 32-bit elements; how exact they have to be, the bound alone decides.
No kernel may reach another device: no remote copies, remote signals or barrier semaphores. Data moves between devices by JAX's collectives and lax.ppermute only.
A program may use at most 64 MiB of HBM per device.

```python
import jax
import jax.numpy as jnp
from jax import lax

B = 256
CT = 2
NT = 64
RT = 4
N_ROW = 16
N_COL = 32


def draw_matrix(key, part):
    key = jax.random.fold_in(key, 11)
    key_sym, key_diag, key_off = jax.random.split(key, 3)
    uniform_part = jax.random.uniform(key_sym, (NT, B, B), jnp.float32, -1.0, 1.0)
    symmetric = (uniform_part + uniform_part.transpose(0, 2, 1)) * 0.55
    diagonal_part = jax.random.uniform(key_diag, (NT, B), jnp.float32, 40.0, 64.0)
    identity = jnp.eye(B, dtype=jnp.float32)
    diag_blocks = symmetric + identity[None] * diagonal_part[:, :, None]
    off_tiles = jnp.clip(0.4 * jax.random.normal(key_off, (NT, B, NT, B), jnp.float32), -1.0, 1.0)
    same_tile = jnp.arange(NT)[:, None, None, None] == jnp.arange(NT)[None, None, :, None]
    assembled = jnp.where(same_tile, diag_blocks[:, :, None, :], off_tiles)
    return assembled.reshape(RT, N_ROW, B, CT, N_COL, B)


def draw_precision(key, part):
    key = jax.random.fold_in(key, 12)
    key_near, key_far = jax.random.split(key)
    near_band = jax.random.randint(key_near, (NT,), 1, 4)
    far_band = near_band + jax.random.randint(key_far, (NT,), 3 * NT // 4, NT + 1)
    distance = jnp.arange(NT)[:, None] - jnp.arange(NT)[None, :]
    levels = jnp.where(distance < 0, 0, jnp.where(distance < near_band[None, :], 2, jnp.where(distance < far_band[None, :], 1, 0)))
    return levels.astype(jnp.int32).reshape(RT, N_ROW, CT, N_COL)


def setup_inputs(seed: int = 0) -> dict:
    seeds = jax.random.split(jax.random.key(seed), 4)
    matrix = draw_matrix(jax.random.fold_in(seeds[3], 71), 0)
    precision = draw_precision(jax.random.fold_in(seeds[3], 71), 0)
    first_col = jax.random.randint(seeds[2], (1,), 0, NT - N_COL // 2 - 1).astype(jnp.int32)
    return {"matrix": matrix, "precision": precision, "first_col": first_col}


def to_bfloat(values):
    narrow = lax.optimization_barrier(values.astype(jnp.bfloat16))
    return narrow.astype(jnp.float32)

def by_level(values, levels):
    shaped = levels.reshape(levels.shape + (1, 1))
    return jnp.where(shaped == 2, values, jnp.where(shaped == 1, to_bfloat(values), 0.0))

def reference(matrix, precision, first_col):
    blocks = matrix.reshape(NT, B, NT, B).transpose(0, 2, 1, 3)
    levels = precision.reshape(NT, NT)
    blocks = by_level(blocks, levels)
    indices = jnp.arange(NT, dtype=jnp.int32)
    zero_at = jnp.zeros((), jnp.int32)
    for step_at in range(2):
        column = (first_col[0] + step_at).astype(jnp.int32)
        diagonal = lax.dynamic_slice(blocks, (column, column, zero_at, zero_at), (1, 1, B, B))[0, 0]
        factor = jnp.linalg.cholesky(diagonal)
        panel_in = lax.dynamic_slice(blocks, (zero_at, column, zero_at, zero_at), (NT, 1, B, B))[:, 0]
        column_levels = lax.dynamic_slice(levels, (zero_at, column), (NT, 1))[:, 0]
        stacked = panel_in.reshape(NT * B, B)
        solved = jax.scipy.linalg.solve_triangular(factor, stacked.T, lower=True).T.reshape(NT, B, B)
        below_mask = (indices > column).reshape(NT, 1, 1)
        lower_rows = jnp.where(below_mask, by_level(solved, column_levels), 0.0)
        on_diag = (indices == column).reshape(NT, 1, 1)
        new_column = jnp.where(below_mask, lower_rows, jnp.where(on_diag, factor, panel_in))
        blocks = lax.dynamic_update_slice(blocks, new_column[:, None], (zero_at, column, zero_at, zero_at))
        narrow_rows = to_bfloat(lower_rows)

        def one_row(row_item, column=column, lower_rows=lower_rows, narrow_rows=narrow_rows):
            row_blocks, row_levels, left_block, narrow_left, row_index = row_item
            precise = jnp.einsum('ab,jcb->jac', left_block, lower_rows, precision=lax.Precision.HIGHEST)
            rounded = jnp.einsum('ab,jcb->jac', narrow_left, narrow_rows, precision=lax.Precision.HIGHEST)
            active = (row_index >= indices) & (indices > column)
            take_precise = (active & (row_levels == 2)).reshape(NT, 1, 1)
            take_rounded = (active & (row_levels == 1)).reshape(NT, 1, 1)
            return jnp.where(take_precise, row_blocks - precise, jnp.where(take_rounded, to_bfloat(row_blocks - rounded), row_blocks))
        blocks = lax.map(one_row, (blocks, levels, lower_rows, narrow_rows, indices))
    return blocks.transpose(0, 2, 1, 3).reshape(RT, N_ROW, B, CT, N_COL, B)
```

```python
import jax
import jax.numpy as jnp
from jax import lax
from jax.experimental import pallas as pl
from jax.experimental.pallas import tpu as pltpu
from jax.sharding import PartitionSpec as P

HIGHEST = lax.Precision.HIGHEST
f32 = jnp.float32
N_ROW = 16
N_COL = 32
B = 256
HALF = 128
SMEM = pl.BlockSpec(memory_space=pltpu.SMEM)
VMEM = pl.BlockSpec(memory_space=pltpu.VMEM)


def dot_nt(a, b):
    return lax.dot_general(
        a, b, (((1,), (1,)), ((), ())), precision=HIGHEST, preferred_element_type=f32
    )


def dot_nn(a, b):
    return lax.dot_general(
        a, b, (((1,), (0,)), ((), ())), precision=HIGHEST, preferred_element_type=f32
    )


def dot_narrow(a, b):
    return lax.dot_general(
        a.astype(jnp.bfloat16),
        b.astype(jnp.bfloat16),
        (((1,), (1,)), ((), ())),
        preferred_element_type=f32,
    )


def rounded(x):
    return x.astype(jnp.bfloat16).astype(f32)


def by_level(x, level):
    return jnp.where(level == 2, x, jnp.where(level == 1, rounded(x), 0.0))


def pack_kernel(scal, prec, mat_ref, out_ref):
    k, q = scal[0], scal[2]
    col = jnp.where(q == k % N_COL, k // N_COL, (k + 1) // N_COL)
    sub = lax.broadcasted_iota(jnp.int32, (8, HALF), 0)
    levels = jnp.zeros((8, HALF), f32)
    for r in range(4):
        level = prec[r, col]
        levels = jnp.where(sub % 4 == r, level.astype(f32), levels)
        for h in range(2):
            rows = mat_ref[pl.ds(r * 1024 + col * 2 + h, B, stride=4), :]
            out_ref[:, r * 2 + h] = by_level(rows, level).reshape(32, 8, HALF)
    out_ref[:, 8] = jnp.broadcast_to(levels[None], (32, 8, HALF))


def pack(scal, prec, mat):
    return pl.pallas_call(
        pack_kernel,
        in_specs=[SMEM, SMEM, VMEM],
        out_specs=VMEM,
        out_shape=jax.ShapeDtypeStruct((N_COL, 9, 8, HALF), f32),
        compiler_params=pltpu.CompilerParams(vmem_limit_bytes=32 << 20),
    )(scal, prec, mat)


def route_kernel(scal, first_ref, second_ref, bulk_ref, even_ref, odd_ref, diag_ref):
    k, p, q = scal[0], scal[1], scal[2]
    low = q < N_ROW
    sub = lax.broadcasted_iota(jnp.int32, (8, HALF), 0)
    for t, ref in enumerate((first_ref, second_ref)):
        for r in range(4):
            for h in range(2):
                bulk_ref[t, r, h] = ref[0, 2 * r + h]
        for c in range(2):
            for h in range(2):
                even = ref[0, 4 * c + h]
                odd = ref[0, 4 * c + 2 + h]
                even_ref[t, c, h] = jnp.where(low, even, odd)
                odd_ref[t, c, h] = jnp.where(low, odd, even)
    next_r = (k + 1) // N_ROW
    here_r = jnp.where(p == k % N_ROW, k // N_ROW, next_r)
    for h in range(2):
        diag_ref[h] = first_ref[0, 2 * here_r + h]
        diag_ref[2 + h] = second_ref[0, 2 * next_r + h]
    diag_ref[4] = jnp.where(sub < 4, first_ref[0, 8], second_ref[0, 8])


def route(scal, received):
    block = (1, 9, 8, HALF)
    return pl.pallas_call(
        route_kernel,
        grid_spec=pltpu.PrefetchScalarGridSpec(
            num_scalar_prefetch=1,
            grid=(1,),
            in_specs=[
                pl.BlockSpec(block, lambda _, s: (s[0] % N_COL, 0, 0, 0)),
                pl.BlockSpec(block, lambda _, s: ((s[0] + 1) % N_COL, 0, 0, 0)),
            ],
            out_specs=[VMEM, VMEM, VMEM, VMEM],
        ),
        out_shape=[
            jax.ShapeDtypeStruct((2, 4, 2, 8, HALF), f32),
            jax.ShapeDtypeStruct((2, 2, 2, 8, HALF), f32),
            jax.ShapeDtypeStruct((2, 2, 2, 8, HALF), f32),
            jax.ShapeDtypeStruct((5, 8, HALF), f32),
        ],
    )(scal, received, received)


def factor_half(block):
    groups = HALF // 8
    sub = lax.broadcasted_iota(jnp.int32, (8, HALF), 0)
    lane = lax.broadcasted_iota(jnp.int32, (8, HALF), 1)
    up = [block[8 * g : 8 * g + 8, :] for g in range(groups)]
    inv = [jnp.where(lane == sub + 8 * g, 1.0, 0.0).astype(f32) for g in range(groups)]
    upper, lower_inv = [], []

    def row(x, j):
        return jnp.broadcast_to(x[j : j + 1, :], (8, HALF))

    def column(x, c):
        return jnp.broadcast_to(x[:, c : c + 1], (8, HALF))

    for b in range(groups):
        rows, irows = up[b], inv[b]
        cols = [column(rows, 8 * b + j) for j in range(8)]
        diag = jnp.zeros((8, HALF), f32)
        for j in range(8):
            pivot = row(cols[j], j)
            recip = 1.0 / pivot
            diag = jnp.where(sub == j, pivot, diag)
            if j < 7:
                mult = jnp.where(sub > j, cols[j] * recip, 0.0)
                for l in range(j + 1, 8):
                    cols[l] = cols[l] - mult * row(cols[l], j)
                rows = rows - mult * row(rows, j)
                irows = irows - mult * row(irows, j)
        scale = lax.rsqrt(diag)
        rows = rows * scale
        irows = irows * scale
        upper.append(jnp.where(lane >= sub + 8 * b, rows, 0.0))
        lower_inv.append(irows)
        if b + 1 < groups:
            row_each = [row(rows, j) for j in range(8)]
            irow_each = [row(irows, j) for j in range(8)]
            flipped = rows.T
            for g in range(b + 1, groups):
                part = flipped[8 * g : 8 * g + 8, :]
                for j in range(8):
                    m = column(part, j)
                    up[g] = up[g] - m * row_each[j]
                    inv[g] = inv[g] - m * irow_each[j]
    return jnp.concatenate(upper, 0), jnp.concatenate(lower_inv, 0)


def factor_kernel(scal, lev, d_ref, l_ref, li_ref, p_ref, s_ref, u_ref, v_ref):
    k = scal[0]

    def tile(n):
        return jnp.concatenate([d_ref[:, 2 * n + h].reshape(B, HALF) for h in range(2)], axis=1)

    s_ref[...] = tile(0)

    def step(t, _):
        def half(h, _):
            at = pl.ds(pl.multiple_of(h * HALF, HALF), HALF)
            u, v = factor_half(s_ref[at, at])
            u_ref[h] = u
            v_ref[h] = v

            @pl.when(h == 0)
            def _():
                l21 = dot_nt(s_ref[HALF:, 0:HALF], v)
                s_ref[HALF:, 0:HALF] = l21
                s_ref[HALF:, HALF:] = s_ref[HALF:, HALF:] - dot_nt(l21, l21)

            return 0

        lax.fori_loop(0, 2, half, 0)
        l21 = s_ref[HALF:, 0:HALF]
        zero = jnp.zeros((HALF, HALF), f32)
        v0, v1 = v_ref[0], v_ref[1]
        l_ref[t, 0:HALF, 0:HALF] = u_ref[0].T
        l_ref[t, 0:HALF, HALF:] = zero
        l_ref[t, HALF:, 0:HALF] = l21
        l_ref[t, HALF:, HALF:] = u_ref[1].T
        li_ref[t, 0:HALF, 0:HALF] = v0
        li_ref[t, 0:HALF, HALF:] = zero
        li_ref[t, HALF:, 0:HALF] = -dot_nn(v1, dot_nn(l21, v0))
        li_ref[t, HALF:, HALF:] = v1

        @pl.when(t == 0)
        def _():
            below = k + 1
            solved = by_level(dot_nt(tile(1), li_ref[0]), lev[below % N_ROW, below // N_ROW])
            p_ref[...] = solved
            s_ref[...] = tile(2) - dot_nt(solved, solved)

        return 0

    lax.fori_loop(0, 2, step, 0)


def factor_two(scal, lev, diag):
    pair = jax.ShapeDtypeStruct((2, B, B), f32)
    return pl.pallas_call(
        factor_kernel,
        in_specs=[SMEM, SMEM, VMEM],
        out_specs=[VMEM] * 3,
        out_shape=[pair, pair, jax.ShapeDtypeStruct((B, B), f32)],
        scratch_shapes=[
            pltpu.VMEM((B, B), f32),
            pltpu.VMEM((2, HALF, HALF), f32),
            pltpu.VMEM((2, HALF, HALF), f32),
        ],
        compiler_params=pltpu.CompilerParams(vmem_limit_bytes=32 << 20),
    )(scal, lev, diag)


def update_kernel(
    scal, lev, prec, rows_ref, cols_ref, l_ref, li_ref, p10_ref, mat_ref, out_ref, panel
):
    k, p, q = scal[0], scal[1], scal[2]

    def level_of(t, i):
        return lev[i % N_ROW, 4 * t + i // N_ROW]

    for t in range(2):
        for r in range(4):
            for h in range(2):
                panel[t, r, :, h * HALF : (h + 1) * HALF] = rows_ref[:, t, r, h].reshape(B, HALF)
        for c in range(2):
            for h in range(2):
                for part in range(2):
                    panel[
                        t, 4 + c, part * HALF : (part + 1) * HALF, h * HALF : (h + 1) * HALF
                    ] = cols_ref[:, part, t, c, h].reshape(HALF, HALF)

    def solve(n, _):
        i = jnp.where(n < 4, n * N_ROW + p, (n - 4) * N_COL + q)

        @pl.when(i > k)
        def _():
            panel[0, n] = by_level(dot_nt(panel[0, n], li_ref[0]), level_of(0, i))
            level = level_of(1, i)

            @pl.when((i > k + 1) & (level == 2))
            def _():
                raw = panel[1, n] - dot_nt(panel[0, n], p10_ref[...])
                panel[1, n] = dot_nt(raw, li_ref[1])

            @pl.when((i > k + 1) & (level == 1))
            def _():
                raw = rounded(panel[1, n] - dot_narrow(panel[0, n], p10_ref[...]))
                panel[1, n] = rounded(dot_nt(raw, li_ref[1]))

        return 0

    lax.fori_loop(0, 6, solve, 0)

    def trail(n, _):
        r, c = n // 2, n % 2
        i = r * N_ROW + p
        j = c * N_COL + q
        level = prec[r, c]
        active = (i >= j) & (j > k)
        halves = [pl.ds(r * 1024 + c * 2 + h, B, stride=4) for h in range(2)]

        def put(value):
            for h in range(2):
                out_ref[halves[h], :] = value[:, h * HALF : (h + 1) * HALF]

        def get():
            return jnp.concatenate([mat_ref[halves[h], :] for h in range(2)], axis=1)

        own_first = (j == k) & (i > k)
        own_second = (j == k + 1) & (i > k + 1)
        diagonal = (i == j) & ((j == k) | (j == k + 1))
        plain = jnp.logical_not(own_first | own_second | diagonal)

        @pl.when(plain & (level == 2))
        def _():
            put(get())

            @pl.when(active)
            def _():
                put(get() - dot_nt(panel[0, r], panel[0, 4 + c]) - dot_nt(panel[1, r], panel[1, 4 + c]))

        @pl.when(plain & (level == 1))
        def _():
            put(rounded(get()))

            @pl.when(active)
            def _():
                once = rounded(rounded(get()) - dot_narrow(panel[0, r], panel[0, 4 + c]))
                put(rounded(once - dot_narrow(panel[1, r], panel[1, 4 + c])))

        @pl.when(plain & (level == 0))
        def _():
            put(jnp.zeros((B, B), f32))

        @pl.when(own_first)
        def _():
            put(panel[0, r])

        @pl.when(own_second)
        def _():
            put(panel[1, r])

        @pl.when(diagonal)
        def _():
            put(l_ref[j - k])

        return 0

    lax.fori_loop(0, 8, trail, 0)


def update(scal, lev, prec, row_tiles, col_tiles, factors, inverses, p10, mat):
    return pl.pallas_call(
        update_kernel,
        in_specs=[SMEM, SMEM, SMEM] + [VMEM] * 6,
        out_specs=VMEM,
        out_shape=jax.ShapeDtypeStruct(mat.shape, f32),
        scratch_shapes=[pltpu.VMEM((2, 6, B, B), f32)],
        compiler_params=pltpu.CompilerParams(vmem_limit_bytes=40 << 20),
    )(scal, lev, prec, row_tiles, col_tiles, factors, inverses, p10, mat)


def cross_pairs(odd):
    pairs = []
    for p in range(N_ROW):
        for q in range(N_COL):
            low = q < N_ROW
            first = low != odd
            row = q if low else q - N_ROW
            col = p if first else p + N_ROW
            pairs.append((p * N_COL + q, row * N_COL + col))
    return pairs


def per_device(matrix, precision, first_col):
    p = lax.axis_index("row")
    q = lax.axis_index("col")
    k = first_col[0]
    scal = jnp.stack([k, p, q]).astype(jnp.int32)
    prec = precision.reshape(4, 2)
    mat = matrix.reshape(4096, HALF)

    sent = pack(scal, prec, mat)
    received = lax.all_to_all(sent, "col", 0, 0)
    bulk, even, odd, diag = route(scal, received)

    row_tiles = lax.all_gather(bulk, "col")
    seen = lax.all_gather(diag, "row")
    both = ("row", "col")
    first = lax.ppermute(even, both, cross_pairs(False))
    second = lax.ppermute(odd, both, cross_pairs(True))
    low = q < N_ROW
    parts = jnp.stack([jnp.where(low, first, second), jnp.where(low, second, first)])
    col_tiles = lax.all_gather(parts, "row")

    lev = seen[:, 4, :, 0].astype(jnp.int32)
    here = lax.dynamic_slice(seen, (k % N_ROW, 0, 0, 0), (1, 2, 8, HALF))[0]
    below = lax.dynamic_slice(seen, ((k + 1) % N_ROW, 0, 0, 0), (1, 4, 8, HALF))[0]
    mine = jnp.concatenate([here, below])
    diags = lax.all_to_all(
        jnp.broadcast_to(mine[None], (N_COL, 6, 8, HALF)), "col", 0, 0
    )
    factors, inverses, p10 = factor_two(scal, lev, diags)
    out = update(scal, lev, prec, row_tiles, col_tiles, factors, inverses, p10, mat)
    return out.reshape(matrix.shape)


def solution(mesh):
    in_specs = (P(None, "row", None, None, "col", None), P(None, "row", None, "col"), P())
    out_specs = P(None, "row", None, None, "col", None)
    return jax.shard_map(
        per_device, mesh=mesh, in_specs=in_specs, out_specs=out_specs, check_vma=False
    )
```

```python
import jax
import jax.numpy as jnp
from jax import lax
from jax.experimental import pallas as pl
from jax.experimental.pallas import tpu as pltpu
from jax.sharding import PartitionSpec as P

HIGHEST = lax.Precision.HIGHEST
f32 = jnp.float32
N_ROW = 16
N_COL = 32
B = 256
HALF = 128
SMEM = pl.BlockSpec(memory_space=pltpu.SMEM)
VMEM = pl.BlockSpec(memory_space=pltpu.VMEM)


def dot_nt(a, b):
    return lax.dot_general(
        a, b, (((1,), (1,)), ((), ())), precision=HIGHEST, preferred_element_type=f32
    )


def dot_nn(a, b):
    return lax.dot_general(
        a, b, (((1,), (0,)), ((), ())), precision=HIGHEST, preferred_element_type=f32
    )


def dot_narrow(a, b):
    return lax.dot_general(
        a.astype(jnp.bfloat16),
        b.astype(jnp.bfloat16),
        (((1,), (1,)), ((), ())),
        preferred_element_type=f32,
    )


def rounded(x):
    return x.astype(jnp.bfloat16).astype(f32)


def by_level(x, level):
    return jnp.where(level == 2, x, jnp.where(level == 1, rounded(x), 0.0))


def pack_kernel(scal, prec, mat_ref, diag_ref, bulk_ref):
    k, p, q = scal[0], scal[1], scal[2]
    col = jnp.where(q == k % N_COL, k // N_COL, (k + 1) // N_COL)
    here_r = jnp.where(p == k % N_ROW, k // N_ROW, (k + 1) // N_ROW)
    sub = lax.broadcasted_iota(jnp.int32, (8, HALF), 0)
    levels = jnp.zeros((8, HALF), f32)
    for r in range(4):
        level = prec[r, col]
        levels = jnp.where(sub % 4 == r, level.astype(f32), levels)
        for h in range(2):
            rows = mat_ref[pl.ds(r * 1024 + col * 2 + h, B, stride=4), :]
            rows = by_level(rows, level).reshape(32, 8, HALF)
            bulk_ref[:, r * 2 + h] = rows

            @pl.when(here_r == r)
            def _():
                diag_ref[:, h] = rows

    diag_ref[:, 2] = jnp.broadcast_to(levels[None], (32, 8, HALF))


def pack(scal, prec, mat):
    return pl.pallas_call(
        pack_kernel,
        in_specs=[SMEM, SMEM, VMEM],
        out_specs=[VMEM, VMEM],
        out_shape=[
            jax.ShapeDtypeStruct((N_COL, 3, 8, HALF), f32),
            jax.ShapeDtypeStruct((N_COL, 8, 8, HALF), f32),
        ],
        compiler_params=pltpu.CompilerParams(vmem_limit_bytes=8 << 20),
    )(scal, prec, mat)


def diag_kernel(scal, first_ref, second_ref, out_ref):
    k, p = scal[0], scal[1]
    sub = lax.broadcasted_iota(jnp.int32, (8, HALF), 0)
    out_ref[0:2] = first_ref[0, 0:2]
    out_ref[2:4] = second_ref[0, 0:2]
    out_ref[4] = jnp.where(sub < 4, first_ref[0, 2], second_ref[0, 2])


def diag_parts(scal, received):
    block = (1, 3, 8, HALF)
    return pl.pallas_call(
        diag_kernel,
        grid_spec=pltpu.PrefetchScalarGridSpec(
            num_scalar_prefetch=1,
            grid=(1,),
            in_specs=[
                pl.BlockSpec(block, lambda _, s: (s[0] % N_COL, 0, 0, 0)),
                pl.BlockSpec(block, lambda _, s: ((s[0] + 1) % N_COL, 0, 0, 0)),
            ],
            out_specs=VMEM,
        ),
        out_shape=jax.ShapeDtypeStruct((5, 8, HALF), f32),
    )(scal, received, received)


def copies_kernel(scal, here_ref, below_ref, out_ref):
    out_ref[:, 0:2] = jnp.broadcast_to(here_ref[:, 0:2], (N_COL, 2, 8, HALF))
    out_ref[:, 2:6] = jnp.broadcast_to(below_ref[:, 0:4], (N_COL, 4, 8, HALF))


def diag_copies(scal, seen):
    block = (1, 5, 8, HALF)
    return pl.pallas_call(
        copies_kernel,
        grid_spec=pltpu.PrefetchScalarGridSpec(
            num_scalar_prefetch=1,
            grid=(1,),
            in_specs=[
                pl.BlockSpec(block, lambda _, s: (s[0] % N_ROW, 0, 0, 0)),
                pl.BlockSpec(block, lambda _, s: ((s[0] + 1) % N_ROW, 0, 0, 0)),
            ],
            out_specs=VMEM,
        ),
        out_shape=jax.ShapeDtypeStruct((N_COL, 6, 8, HALF), f32),
    )(scal, seen, seen)


def route_kernel(scal, first_ref, second_ref, bulk_ref, even_ref, odd_ref):
    low = scal[2] < N_ROW
    for t, ref in enumerate((first_ref, second_ref)):
        for r in range(4):
            for h in range(2):
                part = ref[0, 2 * r + h]
                for z in range(8):
                    bulk_ref[z, t, r, h] = part
        for c in range(2):
            for h in range(2):
                even = ref[0, 4 * c + h]
                odd = ref[0, 4 * c + 2 + h]
                even_ref[t, c, h] = jnp.where(low, even, odd)
                odd_ref[t, c, h] = jnp.where(low, odd, even)


def route(scal, received):
    block = (1, 8, 8, HALF)
    return pl.pallas_call(
        route_kernel,
        grid_spec=pltpu.PrefetchScalarGridSpec(
            num_scalar_prefetch=1,
            grid=(1,),
            in_specs=[
                pl.BlockSpec(block, lambda _, s: (s[0] % N_COL, 0, 0, 0)),
                pl.BlockSpec(block, lambda _, s: ((s[0] + 1) % N_COL, 0, 0, 0)),
            ],
            out_specs=[VMEM, VMEM, VMEM],
        ),
        out_shape=[
            jax.ShapeDtypeStruct((8, 2, 4, 2, 8, HALF), f32),
            jax.ShapeDtypeStruct((2, 2, 2, 8, HALF), f32),
            jax.ShapeDtypeStruct((2, 2, 2, 8, HALF), f32),
        ],
    )(scal, received, received)


def cols_kernel(scal, first_ref, second_ref, out_ref):
    low = scal[2] < N_ROW
    first, second = first_ref[...], second_ref[...]
    lo = jnp.where(low, first, second)
    hi = jnp.where(low, second, first)
    for y in range(N_ROW):
        out_ref[y, 0] = lo
        out_ref[y, 1] = hi


def col_copies(scal, first, second):
    return pl.pallas_call(
        cols_kernel,
        in_specs=[SMEM, VMEM, VMEM],
        out_specs=VMEM,
        out_shape=jax.ShapeDtypeStruct((N_ROW, 2, 2, 2, 2, 8, HALF), f32),
    )(scal, first, second)


def factor_half(block):
    groups = HALF // 8
    sub = lax.broadcasted_iota(jnp.int32, (8, HALF), 0)
    lane = lax.broadcasted_iota(jnp.int32, (8, HALF), 1)
    up = [block[8 * g : 8 * g + 8, :] for g in range(groups)]
    inv = [jnp.where(lane == sub + 8 * g, 1.0, 0.0).astype(f32) for g in range(groups)]
    upper, lower_inv = [], []

    def row(x, j):
        return jnp.broadcast_to(x[j : j + 1, :], (8, HALF))

    def column(x, c):
        return jnp.broadcast_to(x[:, c : c + 1], (8, HALF))

    for b in range(groups):
        rows, irows = up[b], inv[b]
        cols = [column(rows, 8 * b + j) for j in range(8)]
        diag = jnp.zeros((8, HALF), f32)
        for j in range(8):
            pivot = row(cols[j], j)
            recip = 1.0 / pivot
            diag = jnp.where(sub == j, pivot, diag)
            if j < 7:
                mult = jnp.where(sub > j, cols[j] * recip, 0.0)
                for l in range(j + 1, 8):
                    cols[l] = cols[l] - mult * row(cols[l], j)
                rows = rows - mult * row(rows, j)
                irows = irows - mult * row(irows, j)
        scale = lax.rsqrt(diag)
        rows = rows * scale
        irows = irows * scale
        upper.append(jnp.where(lane >= sub + 8 * b, rows, 0.0))
        lower_inv.append(irows)
        if b + 1 < groups:
            row_each = [row(rows, j) for j in range(8)]
            irow_each = [row(irows, j) for j in range(8)]
            flipped = rows.T
            for g in range(b + 1, groups):
                part = flipped[8 * g : 8 * g + 8, :]
                for j in range(8):
                    m = column(part, j)
                    up[g] = up[g] - m * row_each[j]
                    inv[g] = inv[g] - m * irow_each[j]
    return jnp.concatenate(upper, 0), jnp.concatenate(lower_inv, 0)


def factor_kernel(scal, lev, d_ref, l_ref, li_ref, p_ref, s_ref, u_ref, v_ref):
    k = scal[0]

    def tile(n):
        return jnp.concatenate([d_ref[:, 2 * n + h].reshape(B, HALF) for h in range(2)], axis=1)

    s_ref[...] = tile(0)

    def step(t, _):
        def half(h, _):
            at = pl.ds(pl.multiple_of(h * HALF, HALF), HALF)
            u, v = factor_half(s_ref[at, at])
            u_ref[h] = u
            v_ref[h] = v

            @pl.when(h == 0)
            def _():
                l21 = dot_nt(s_ref[HALF:, 0:HALF], v)
                s_ref[HALF:, 0:HALF] = l21
                s_ref[HALF:, HALF:] = s_ref[HALF:, HALF:] - dot_nt(l21, l21)

            return 0

        lax.fori_loop(0, 2, half, 0)
        l21 = s_ref[HALF:, 0:HALF]
        zero = jnp.zeros((HALF, HALF), f32)
        v0, v1 = v_ref[0], v_ref[1]
        l_ref[t, 0:HALF, 0:HALF] = u_ref[0].T
        l_ref[t, 0:HALF, HALF:] = zero
        l_ref[t, HALF:, 0:HALF] = l21
        l_ref[t, HALF:, HALF:] = u_ref[1].T
        li_ref[t, 0:HALF, 0:HALF] = v0
        li_ref[t, 0:HALF, HALF:] = zero
        li_ref[t, HALF:, 0:HALF] = -dot_nn(v1, dot_nn(l21, v0))
        li_ref[t, HALF:, HALF:] = v1

        @pl.when(t == 0)
        def _():
            below = k + 1
            solved = by_level(dot_nt(tile(1), li_ref[0]), lev[below % N_ROW, below // N_ROW])
            p_ref[...] = solved
            s_ref[...] = tile(2) - dot_nt(solved, solved)

        return 0

    lax.fori_loop(0, 2, step, 0)


def factor_two(scal, lev, diag):
    pair = jax.ShapeDtypeStruct((2, B, B), f32)
    return pl.pallas_call(
        factor_kernel,
        in_specs=[SMEM, SMEM, VMEM],
        out_specs=[VMEM] * 3,
        out_shape=[pair, pair, jax.ShapeDtypeStruct((B, B), f32)],
        scratch_shapes=[
            pltpu.VMEM((B, B), f32),
            pltpu.VMEM((2, HALF, HALF), f32),
            pltpu.VMEM((2, HALF, HALF), f32),
        ],
        compiler_params=pltpu.CompilerParams(vmem_limit_bytes=8 << 20),
        cost_estimate=pl.CostEstimate(flops=3 * 10**10, bytes_accessed=10**6, transcendentals=0),
    )(scal, lev, diag)


def update_kernel(
    scal, lev, prec, rows_ref, cols_ref, l_ref, li_ref, p10_ref, mat_ref, out_ref, panel
):
    k, p, q = scal[0], scal[1], scal[2]

    def level_of(t, i):
        return lev[i % N_ROW, 4 * t + i // N_ROW]

    for t in range(2):
        for h in range(2):
            lanes = slice(h * HALF, (h + 1) * HALF)
            for r in range(4):
                for x in range(4):
                    for z in range(8):
                        at = 8 * (4 * z + x)
                        panel[t, r, at : at + 8, lanes] = rows_ref[x, z, t, r, h]
            for c in range(2):
                for part in range(2):
                    at = slice(part * HALF, (part + 1) * HALF)
                    panel[t, 4 + c, at, lanes] = cols_ref[:, part, t, c, h].reshape(HALF, HALF)

    def solve(n, _):
        i = jnp.where(n < 4, n * N_ROW + p, (n - 4) * N_COL + q)

        @pl.when(i > k)
        def _():
            panel[0, n] = by_level(dot_nt(panel[0, n], li_ref[0]), level_of(0, i))
            level = level_of(1, i)

            @pl.when((i > k + 1) & (level == 2))
            def _():
                raw = panel[1, n] - dot_nt(panel[0, n], p10_ref[...])
                panel[1, n] = dot_nt(raw, li_ref[1])

            @pl.when((i > k + 1) & (level == 1))
            def _():
                raw = rounded(panel[1, n] - dot_narrow(panel[0, n], p10_ref[...]))
                panel[1, n] = rounded(dot_nt(raw, li_ref[1]))

        return 0

    lax.fori_loop(0, 6, solve, 0)

    def trail(n, _):
        r, c = n // 2, n % 2
        i = r * N_ROW + p
        j = c * N_COL + q
        level = prec[r, c]
        active = (i >= j) & (j > k)
        halves = [pl.ds(r * 1024 + c * 2 + h, B, stride=4) for h in range(2)]

        def put(value):
            for h in range(2):
                out_ref[halves[h], :] = value[:, h * HALF : (h + 1) * HALF]

        def get():
            return jnp.concatenate([mat_ref[halves[h], :] for h in range(2)], axis=1)

        own_first = (j == k) & (i > k)
        own_second = (j == k + 1) & (i > k + 1)
        diagonal = (i == j) & ((j == k) | (j == k + 1))
        plain = jnp.logical_not(own_first | own_second | diagonal)

        @pl.when(plain & (level == 2))
        def _():
            put(get())

            @pl.when(active)
            def _():
                put(get() - dot_nt(panel[0, r], panel[0, 4 + c]) - dot_nt(panel[1, r], panel[1, 4 + c]))

        @pl.when(plain & (level == 1))
        def _():
            put(rounded(get()))

            @pl.when(active)
            def _():
                once = rounded(rounded(get()) - dot_narrow(panel[0, r], panel[0, 4 + c]))
                put(rounded(once - dot_narrow(panel[1, r], panel[1, 4 + c])))

        @pl.when(plain & (level == 0))
        def _():
            put(jnp.zeros((B, B), f32))

        @pl.when(own_first)
        def _():
            put(panel[0, r])

        @pl.when(own_second)
        def _():
            put(panel[1, r])

        @pl.when(diagonal)
        def _():
            put(l_ref[j - k])

        return 0

    lax.fori_loop(0, 8, trail, 0)


def update(scal, lev, prec, row_tiles, col_tiles, factors, inverses, p10, mat):
    return pl.pallas_call(
        update_kernel,
        in_specs=[SMEM, SMEM, SMEM] + [VMEM] * 6,
        out_specs=VMEM,
        out_shape=jax.ShapeDtypeStruct(mat.shape, f32),
        scratch_shapes=[pltpu.VMEM((2, 6, B, B), f32)],
        compiler_params=pltpu.CompilerParams(vmem_limit_bytes=12 << 20),
        cost_estimate=pl.CostEstimate(flops=10**10, bytes_accessed=10**7, transcendentals=0),
    )(scal, lev, prec, row_tiles, col_tiles, factors, inverses, p10, mat)


def cross_pairs(odd):
    pairs = []
    for p in range(N_ROW):
        for q in range(N_COL):
            low = q < N_ROW
            first = low != odd
            row = q if low else q - N_ROW
            col = p if first else p + N_ROW
            pairs.append((p * N_COL + q, row * N_COL + col))
    return pairs


def per_device(matrix, precision, first_col):
    p = lax.axis_index("row")
    q = lax.axis_index("col")
    k = first_col[0]
    scal = jnp.stack([k, p, q]).astype(jnp.int32)
    prec = precision.reshape(4, 2)
    mat = matrix.reshape(4096, HALF)

    z_groups = [[4 * z + x for z in range(8)] for x in range(4)]
    x_groups = [[4 * z + x for x in range(4)] for z in range(8)]

    sent_diag, sent_bulk = pack(scal, prec, mat)
    got_diag = lax.all_to_all(sent_diag, "col", 0, 0)
    seen = lax.all_gather(diag_parts(scal, got_diag), "row")
    got_bulk = lax.all_to_all(sent_bulk, "col", 0, 0)
    bulk, even, odd = route(scal, got_bulk)
    diags = lax.all_to_all(diag_copies(scal, seen), "col", 0, 0)
    lev = seen[:, 4, :, 0].astype(jnp.int32)

    both = ("row", "col")
    first = lax.ppermute(even, both, cross_pairs(False))
    second = lax.ppermute(odd, both, cross_pairs(True))
    slab = lax.all_to_all(bulk, "col", 0, 0, axis_index_groups=z_groups)
    diags, first, second, slab = lax.optimization_barrier((diags, first, second, slab))

    col_tiles = lax.all_to_all(col_copies(scal, first, second), "row", 0, 0)
    row_tiles = lax.all_to_all(
        jnp.broadcast_to(slab[None], (4,) + slab.shape), "col", 0, 0, axis_index_groups=x_groups
    )
    factors, inverses, p10 = factor_two(scal, lev, diags)
    out = update(
        scal, lev, prec, row_tiles, col_tiles, factors, inverses, p10, mat
    )
    return out.reshape(matrix.shape)


def solution(mesh):
    in_specs = (P(None, "row", None, None, "col", None), P(None, "row", None, "col"), P())
    out_specs = P(None, "row", None, None, "col", None)
    return jax.shard_map(
        per_device, mesh=mesh, in_specs=in_specs, out_specs=out_specs, check_vma=False
    )
```

```python
import jax
import jax.numpy as jnp
from jax import lax
from jax.experimental import pallas as pl
from jax.experimental.pallas import tpu as pltpu
from jax.sharding import PartitionSpec as P

HIGHEST = lax.Precision.HIGHEST
f32 = jnp.float32
N_ROW = 16
N_COL = 32
B = 256
HALF = 128
SMEM = pl.BlockSpec(memory_space=pltpu.SMEM)
VMEM = pl.BlockSpec(memory_space=pltpu.VMEM)


def dot_nt(a, b):
    return lax.dot_general(
        a, b, (((1,), (1,)), ((), ())), precision=HIGHEST, preferred_element_type=f32
    )


def dot_nn(a, b):
    return lax.dot_general(
        a, b, (((1,), (0,)), ((), ())), precision=HIGHEST, preferred_element_type=f32
    )


def dot_narrow(a, b):
    return lax.dot_general(
        a.astype(jnp.bfloat16),
        b.astype(jnp.bfloat16),
        (((1,), (1,)), ((), ())),
        preferred_element_type=f32,
    )


def rounded(x):
    return x.astype(jnp.bfloat16).astype(f32)


def by_level(x, level):
    return jnp.where(level == 2, x, jnp.where(level == 1, rounded(x), 0.0))


def pack_kernel(scal, prec, mat_ref, diag_ref, bulk_ref):
    k, p, q = scal[0], scal[1], scal[2]
    col = jnp.where(q == k % N_COL, k // N_COL, (k + 1) // N_COL)
    here_r = jnp.where(p == k % N_ROW, k // N_ROW, (k + 1) // N_ROW)
    sub = lax.broadcasted_iota(jnp.int32, (8, HALF), 0)
    levels = jnp.zeros((8, HALF), f32)
    for r in range(4):
        level = prec[r, col]
        levels = jnp.where(sub % 4 == r, level.astype(f32), levels)
        for h in range(2):
            rows = mat_ref[pl.ds(r * 1024 + col * 2 + h, B, stride=4), :]
            rows = by_level(rows, level).reshape(32, 8, HALF)
            bulk_ref[:, r * 2 + h] = rows

            @pl.when(here_r == r)
            def _():
                diag_ref[:, h] = rows

    diag_ref[:, 2] = jnp.broadcast_to(levels[None], (32, 8, HALF))


def pack(scal, prec, mat):
    return pl.pallas_call(
        pack_kernel,
        in_specs=[SMEM, SMEM, VMEM],
        out_specs=[VMEM, VMEM],
        out_shape=[
            jax.ShapeDtypeStruct((N_COL, 3, 8, HALF), f32),
            jax.ShapeDtypeStruct((N_COL, 8, 8, HALF), f32),
        ],
        compiler_params=pltpu.CompilerParams(vmem_limit_bytes=8 << 20),
    )(scal, prec, mat)


def diag_kernel(scal, first_ref, second_ref, out_ref):
    k, p = scal[0], scal[1]
    sub = lax.broadcasted_iota(jnp.int32, (8, HALF), 0)
    out_ref[0:2] = first_ref[0, 0:2]
    out_ref[2:4] = second_ref[0, 0:2]
    out_ref[4] = jnp.where(sub < 4, first_ref[0, 2], second_ref[0, 2])


def diag_parts(scal, received):
    block = (1, 3, 8, HALF)
    return pl.pallas_call(
        diag_kernel,
        grid_spec=pltpu.PrefetchScalarGridSpec(
            num_scalar_prefetch=1,
            grid=(1,),
            in_specs=[
                pl.BlockSpec(block, lambda _, s: (s[0] % N_COL, 0, 0, 0)),
                pl.BlockSpec(block, lambda _, s: ((s[0] + 1) % N_COL, 0, 0, 0)),
            ],
            out_specs=VMEM,
        ),
        out_shape=jax.ShapeDtypeStruct((5, 8, HALF), f32),
    )(scal, received, received)


def choose_kernel(scal, here_ref, below_ref, out_ref):
    out_ref[0:2] = here_ref[0, 0:2]
    out_ref[2:6] = below_ref[0, 0:4]


def diag_choice(scal, seen):
    block = (1, 5, 8, HALF)
    return pl.pallas_call(
        choose_kernel,
        grid_spec=pltpu.PrefetchScalarGridSpec(
            num_scalar_prefetch=1,
            grid=(1,),
            in_specs=[
                pl.BlockSpec(block, lambda _, s: (s[0] % N_ROW, 0, 0, 0)),
                pl.BlockSpec(block, lambda _, s: ((s[0] + 1) % N_ROW, 0, 0, 0)),
            ],
            out_specs=VMEM,
        ),
        out_shape=jax.ShapeDtypeStruct((6, 8, HALF), f32),
    )(scal, seen, seen)


def route_kernel(scal, first_ref, second_ref, bulk_ref, even_ref, odd_ref):
    low = scal[2] < N_ROW
    for t, ref in enumerate((first_ref, second_ref)):
        for r in range(4):
            for h in range(2):
                bulk_ref[t, r, h] = ref[0, 2 * r + h]
        for c in range(2):
            for h in range(2):
                even = ref[0, 4 * c + h]
                odd = ref[0, 4 * c + 2 + h]
                even_ref[t, c, h] = jnp.where(low, even, odd)
                odd_ref[t, c, h] = jnp.where(low, odd, even)


def route(scal, received):
    block = (1, 8, 8, HALF)
    return pl.pallas_call(
        route_kernel,
        grid_spec=pltpu.PrefetchScalarGridSpec(
            num_scalar_prefetch=1,
            grid=(1,),
            in_specs=[
                pl.BlockSpec(block, lambda _, s: (s[0] % N_COL, 0, 0, 0)),
                pl.BlockSpec(block, lambda _, s: ((s[0] + 1) % N_COL, 0, 0, 0)),
            ],
            out_specs=[VMEM, VMEM, VMEM],
        ),
        out_shape=[
            jax.ShapeDtypeStruct((2, 4, 2, 8, HALF), f32),
            jax.ShapeDtypeStruct((2, 2, 2, 8, HALF), f32),
            jax.ShapeDtypeStruct((2, 2, 2, 8, HALF), f32),
        ],
    )(scal, received, received)


def cols_kernel(scal, first_ref, second_ref, out_ref):
    low = scal[2] < N_ROW
    first, second = first_ref[...], second_ref[...]
    out_ref[0] = jnp.where(low, first, second)
    out_ref[1] = jnp.where(low, second, first)


def order_cols(scal, first, second):
    return pl.pallas_call(
        cols_kernel,
        in_specs=[SMEM, VMEM, VMEM],
        out_specs=VMEM,
        out_shape=jax.ShapeDtypeStruct((2, 2, 2, 2, 8, HALF), f32),
    )(scal, first, second)


def line_kernel(scal, *refs):
    z = scal[2] // 4
    for d in range(8):
        refs[8][(z + 8 - d) % 8] = refs[d][...]


def z_line(scal, part):
    shifts = [
        lax.ppermute(part, "col", [(i, (i + 4 * d) % N_COL) for i in range(N_COL)])
        for d in range(1, 8)
    ]
    return [part] + shifts


def in_order(scal, parts):
    return pl.pallas_call(
        line_kernel,
        in_specs=[SMEM] + [VMEM] * 8,
        out_specs=VMEM,
        out_shape=jax.ShapeDtypeStruct((8,) + parts[0].shape, f32),
    )(scal, *parts)


def x_line(slab):
    shifts = [
        lax.ppermute(slab, "col", [(i, i - i % 4 + (i + d) % 4) for i in range(N_COL)])
        for d in range(1, 4)
    ]
    return [slab] + shifts


def factor_half(block):
    groups = HALF // 8
    sub = lax.broadcasted_iota(jnp.int32, (8, HALF), 0)
    lane = lax.broadcasted_iota(jnp.int32, (8, HALF), 1)
    up = [block[8 * g : 8 * g + 8, :] for g in range(groups)]
    inv = [jnp.where(lane == sub + 8 * g, 1.0, 0.0).astype(f32) for g in range(groups)]
    upper, lower_inv = [], []

    def row(x, j):
        return jnp.broadcast_to(x[j : j + 1, :], (8, HALF))

    def column(x, c):
        return jnp.broadcast_to(x[:, c : c + 1], (8, HALF))

    for b in range(groups):
        rows, irows = up[b], inv[b]
        cols = [column(rows, 8 * b + j) for j in range(8)]
        diag = jnp.zeros((8, HALF), f32)
        for j in range(8):
            pivot = row(cols[j], j)
            recip = 1.0 / pivot
            diag = jnp.where(sub == j, pivot, diag)
            if j < 7:
                mult = jnp.where(sub > j, cols[j] * recip, 0.0)
                for l in range(j + 1, 8):
                    cols[l] = cols[l] - mult * row(cols[l], j)
                rows = rows - mult * row(rows, j)
                irows = irows - mult * row(irows, j)
        scale = lax.rsqrt(diag)
        rows = rows * scale
        irows = irows * scale
        upper.append(jnp.where(lane >= sub + 8 * b, rows, 0.0))
        lower_inv.append(irows)
        if b + 1 < groups:
            row_each = [row(rows, j) for j in range(8)]
            irow_each = [row(irows, j) for j in range(8)]
            flipped = rows.T
            for g in range(b + 1, groups):
                part = flipped[8 * g : 8 * g + 8, :]
                for j in range(8):
                    m = column(part, j)
                    up[g] = up[g] - m * row_each[j]
                    inv[g] = inv[g] - m * irow_each[j]
    return jnp.concatenate(upper, 0), jnp.concatenate(lower_inv, 0)


def factor_kernel(scal, lev, d0, d1, d2, d3, out_ref, d_ref, s_ref, u_ref, v_ref):
    k, x = scal[0], scal[2] % 4
    for d, ref in enumerate((d0, d1, d2, d3)):
        from_x = (x + 4 - d) % 4
        for z in range(8):
            d_ref[4 * z + from_x] = ref[z]

    def tile(n):
        return jnp.concatenate([d_ref[:, 2 * n + h].reshape(B, HALF) for h in range(2)], axis=1)

    s_ref[...] = tile(0)

    def step(t, _):
        def half(h, _):
            at = pl.ds(pl.multiple_of(h * HALF, HALF), HALF)
            u, v = factor_half(s_ref[at, at])
            u_ref[h] = u
            v_ref[h] = v

            @pl.when(h == 0)
            def _():
                l21 = dot_nt(s_ref[HALF:, 0:HALF], v)
                s_ref[HALF:, 0:HALF] = l21
                s_ref[HALF:, HALF:] = s_ref[HALF:, HALF:] - dot_nt(l21, l21)

            return 0

        lax.fori_loop(0, 2, half, 0)
        l21 = s_ref[HALF:, 0:HALF]
        zero = jnp.zeros((HALF, HALF), f32)
        v0, v1 = v_ref[0], v_ref[1]
        out_ref[t, 0:HALF, 0:HALF] = u_ref[0].T
        out_ref[t, 0:HALF, HALF:] = zero
        out_ref[t, HALF:, 0:HALF] = l21
        out_ref[t, HALF:, HALF:] = u_ref[1].T
        out_ref[2 + t, 0:HALF, 0:HALF] = v0
        out_ref[2 + t, 0:HALF, HALF:] = zero
        out_ref[2 + t, HALF:, 0:HALF] = -dot_nn(v1, dot_nn(l21, v0))
        out_ref[2 + t, HALF:, HALF:] = v1

        @pl.when(t == 0)
        def _():
            below = k + 1
            solved = by_level(dot_nt(tile(1), out_ref[2]), lev[below % N_ROW, below // N_ROW])
            out_ref[4] = solved
            s_ref[...] = tile(2) - dot_nt(solved, solved)

        return 0

    lax.fori_loop(0, 2, step, 0)


def factor_two(scal, lev, diags):
    return pl.pallas_call(
        factor_kernel,
        in_specs=[SMEM, SMEM] + [VMEM] * 4,
        out_specs=VMEM,
        out_shape=jax.ShapeDtypeStruct((5, B, B), f32),
        scratch_shapes=[
            pltpu.VMEM((N_COL, 6, 8, HALF), f32),
            pltpu.VMEM((B, B), f32),
            pltpu.VMEM((2, HALF, HALF), f32),
            pltpu.VMEM((2, HALF, HALF), f32),
        ],
        compiler_params=pltpu.CompilerParams(vmem_limit_bytes=8 << 20),
        cost_estimate=pl.CostEstimate(flops=3 * 10**10, bytes_accessed=10**6, transcendentals=0),
    )(scal, lev, *diags)


def update_kernel(
    scal, lev, prec, row0, row1, row2, row3, cols_ref, f_ref, mat_ref, out_ref, panel
):
    k, p, q = scal[0], scal[1], scal[2]
    x = q % 4

    def level_of(t, i):
        return lev[i % N_ROW, 4 * t + i // N_ROW]

    for t in range(2):
        for h in range(2):
            lanes = slice(h * HALF, (h + 1) * HALF)
            for r in range(4):
                for d, ref in enumerate((row0, row1, row2, row3)):
                    for z in range(8):
                        at = pl.ds(pl.multiple_of(32 * z + 8 * ((x + 4 - d) % 4), 8), 8)
                        panel[t, r, at, lanes] = ref[z, t, r, h]
            for c in range(2):
                for part in range(2):
                    at = slice(part * HALF, (part + 1) * HALF)
                    panel[t, 4 + c, at, lanes] = cols_ref[:, part, t, c, h].reshape(HALF, HALF)

    def solve(n, _):
        i = jnp.where(n < 4, n * N_ROW + p, (n - 4) * N_COL + q)

        @pl.when(i > k)
        def _():
            panel[0, n] = by_level(dot_nt(panel[0, n], f_ref[2]), level_of(0, i))
            level = level_of(1, i)

            @pl.when((i > k + 1) & (level == 2))
            def _():
                raw = panel[1, n] - dot_nt(panel[0, n], f_ref[4])
                panel[1, n] = dot_nt(raw, f_ref[3])

            @pl.when((i > k + 1) & (level == 1))
            def _():
                raw = rounded(panel[1, n] - dot_narrow(panel[0, n], f_ref[4]))
                panel[1, n] = rounded(dot_nt(raw, f_ref[3]))

        return 0

    lax.fori_loop(0, 6, solve, 0)

    def trail(n, _):
        r, c = n // 2, n % 2
        i = r * N_ROW + p
        j = c * N_COL + q
        level = prec[r, c]
        active = (i >= j) & (j > k)
        halves = [pl.ds(r * 1024 + c * 2 + h, B, stride=4) for h in range(2)]

        def put(value):
            for h in range(2):
                out_ref[halves[h], :] = value[:, h * HALF : (h + 1) * HALF]

        def get():
            return jnp.concatenate([mat_ref[halves[h], :] for h in range(2)], axis=1)

        own_first = (j == k) & (i > k)
        own_second = (j == k + 1) & (i > k + 1)
        diagonal = (i == j) & ((j == k) | (j == k + 1))
        plain = jnp.logical_not(own_first | own_second | diagonal)

        @pl.when(plain & (level == 2))
        def _():
            put(get())

            @pl.when(active)
            def _():
                put(get() - dot_nt(panel[0, r], panel[0, 4 + c]) - dot_nt(panel[1, r], panel[1, 4 + c]))

        @pl.when(plain & (level == 1))
        def _():
            put(rounded(get()))

            @pl.when(active)
            def _():
                once = rounded(rounded(get()) - dot_narrow(panel[0, r], panel[0, 4 + c]))
                put(rounded(once - dot_narrow(panel[1, r], panel[1, 4 + c])))

        @pl.when(plain & (level == 0))
        def _():
            put(jnp.zeros((B, B), f32))

        @pl.when(own_first)
        def _():
            put(panel[0, r])

        @pl.when(own_second)
        def _():
            put(panel[1, r])

        @pl.when(diagonal)
        def _():
            put(f_ref[j - k])

        return 0

    lax.fori_loop(0, 8, trail, 0)


def update(scal, lev, prec, row_tiles, col_tiles, factors, mat):
    return pl.pallas_call(
        update_kernel,
        in_specs=[SMEM, SMEM, SMEM] + [VMEM] * 7,
        out_specs=VMEM,
        out_shape=jax.ShapeDtypeStruct(mat.shape, f32),
        scratch_shapes=[pltpu.VMEM((2, 6, B, B), f32)],
        compiler_params=pltpu.CompilerParams(vmem_limit_bytes=12 << 20),
        cost_estimate=pl.CostEstimate(flops=10**10, bytes_accessed=10**7, transcendentals=0),
    )(scal, lev, prec, *row_tiles, col_tiles, factors, mat)


def cross_pairs(odd):
    pairs = []
    for p in range(N_ROW):
        for q in range(N_COL):
            low = q < N_ROW
            first = low != odd
            row = q if low else q - N_ROW
            col = p if first else p + N_ROW
            pairs.append((p * N_COL + q, row * N_COL + col))
    return pairs


def per_device(matrix, precision, first_col):
    p = lax.axis_index("row")
    q = lax.axis_index("col")
    k = first_col[0]
    scal = jnp.stack([k, p, q]).astype(jnp.int32)
    prec = precision.reshape(4, 2)
    mat = matrix.reshape(4096, HALF)

    sent_diag, sent_bulk = pack(scal, prec, mat)
    got_diag = lax.all_to_all(sent_diag, "col", 0, 0)
    seen = lax.all_gather(diag_parts(scal, got_diag), "row")
    got_bulk = lax.all_to_all(sent_bulk, "col", 0, 0)
    bulk, even, odd = route(scal, got_bulk)
    lev = seen[:, 4, :, 0].astype(jnp.int32)

    both = ("row", "col")
    first = lax.ppermute(even, both, cross_pairs(False))
    second = lax.ppermute(odd, both, cross_pairs(True))
    col_tiles = lax.all_gather(order_cols(scal, first, second), "row")

    diag_line = z_line(scal, diag_choice(scal, seen))
    diag_slab = in_order(scal, diag_line)
    slab = in_order(scal, z_line(scal, bulk))
    diag_slab, slab = lax.optimization_barrier((diag_slab, slab))
    diags = x_line(diag_slab)
    row_tiles = x_line(slab)
    factors = factor_two(scal, lev, diags)
    out = update(scal, lev, prec, row_tiles, col_tiles, factors, mat)
    return out.reshape(matrix.shape)


def solution(mesh):
    in_specs = (P(None, "row", None, None, "col", None), P(None, "row", None, "col"), P())
    out_specs = P(None, "row", None, None, "col", None)
    return jax.shard_map(
        per_device, mesh=mesh, in_specs=in_specs, out_specs=out_specs, check_vma=False
    )
```

```python
import jax
import jax.numpy as jnp
from jax import lax
from jax.experimental import pallas as pl
from jax.experimental.pallas import tpu as pltpu
from jax.sharding import PartitionSpec as P

HIGHEST = lax.Precision.HIGHEST
f32 = jnp.float32
N_ROW = 16
N_COL = 32
B = 256
HALF = 128
SMEM = pl.BlockSpec(memory_space=pltpu.SMEM)
VMEM = pl.BlockSpec(memory_space=pltpu.VMEM)
HBM = pl.BlockSpec(memory_space=pltpu.HBM)


def dot_nt(a, b):
    return lax.dot_general(
        a, b, (((1,), (1,)), ((), ())), precision=HIGHEST, preferred_element_type=f32
    )


def dot_nn(a, b):
    return lax.dot_general(
        a, b, (((1,), (0,)), ((), ())), precision=HIGHEST, preferred_element_type=f32
    )


def dot_narrow(a, b):
    return lax.dot_general(
        a.astype(jnp.bfloat16),
        b.astype(jnp.bfloat16),
        (((1,), (1,)), ((), ())),
        preferred_element_type=f32,
    )


def rounded(x):
    return x.astype(jnp.bfloat16).astype(f32)


def by_level(x, level):
    return jnp.where(level == 2, x, jnp.where(level == 1, rounded(x), 0.0))


def pack_kernel(scal, prec, mat_ref, diag_ref, bulk_ref):
    k, p, q = scal[0], scal[1], scal[2]
    col = jnp.where(q == k % N_COL, k // N_COL, (k + 1) // N_COL)
    here_r = jnp.where(p == k % N_ROW, k // N_ROW, (k + 1) // N_ROW)
    sub = lax.broadcasted_iota(jnp.int32, (8, HALF), 0)
    levels = jnp.zeros((8, HALF), f32)
    for r in range(4):
        level = prec[r, col]
        levels = jnp.where(sub % 4 == r, level.astype(f32), levels)
        for h in range(2):
            rows = mat_ref[pl.ds(r * 1024 + col * 2 + h, B, stride=4), :]
            rows = by_level(rows, level).reshape(32, 8, HALF)
            bulk_ref[:, r * 2 + h] = rows

            @pl.when(here_r == r)
            def _():
                diag_ref[:, h] = rows

    diag_ref[:, 2] = jnp.broadcast_to(levels[None], (32, 8, HALF))


def pack(scal, prec, mat):
    return pl.pallas_call(
        pack_kernel,
        in_specs=[SMEM, SMEM, VMEM],
        out_specs=[VMEM, VMEM],
        out_shape=[
            jax.ShapeDtypeStruct((N_COL, 3, 8, HALF), f32),
            jax.ShapeDtypeStruct((N_COL, 8, 8, HALF), f32),
        ],
        compiler_params=pltpu.CompilerParams(vmem_limit_bytes=8 << 20),
    )(scal, prec, mat)


def diag_kernel(scal, first_ref, second_ref, out_ref):
    k, p = scal[0], scal[1]
    sub = lax.broadcasted_iota(jnp.int32, (8, HALF), 0)
    out_ref[0:2] = first_ref[0, 0:2]
    out_ref[2:4] = second_ref[0, 0:2]
    out_ref[4] = jnp.where(sub < 4, first_ref[0, 2], second_ref[0, 2])


def diag_parts(scal, received):
    block = (1, 3, 8, HALF)
    return pl.pallas_call(
        diag_kernel,
        grid_spec=pltpu.PrefetchScalarGridSpec(
            num_scalar_prefetch=1,
            grid=(1,),
            in_specs=[
                pl.BlockSpec(block, lambda _, s: (s[0] % N_COL, 0, 0, 0)),
                pl.BlockSpec(block, lambda _, s: ((s[0] + 1) % N_COL, 0, 0, 0)),
            ],
            out_specs=VMEM,
        ),
        out_shape=jax.ShapeDtypeStruct((5, 8, HALF), f32),
    )(scal, received, received)


def copies_kernel(scal, here_ref, below_ref, out_ref):
    out_ref[:, 0:2] = jnp.broadcast_to(here_ref[:, 0:2], (N_COL, 2, 8, HALF))
    out_ref[:, 2:6] = jnp.broadcast_to(below_ref[:, 0:4], (N_COL, 4, 8, HALF))


def diag_copies(scal, seen):
    block = (1, 5, 8, HALF)
    return pl.pallas_call(
        copies_kernel,
        grid_spec=pltpu.PrefetchScalarGridSpec(
            num_scalar_prefetch=1,
            grid=(1,),
            in_specs=[
                pl.BlockSpec(block, lambda _, s: (s[0] % N_ROW, 0, 0, 0)),
                pl.BlockSpec(block, lambda _, s: ((s[0] + 1) % N_ROW, 0, 0, 0)),
            ],
            out_specs=VMEM,
        ),
        out_shape=jax.ShapeDtypeStruct((N_COL, 6, 8, HALF), f32),
    )(scal, seen, seen)


def route_kernel(scal, first_ref, second_ref, bulk_ref, even_ref, odd_ref):
    low = scal[2] < N_ROW
    for t, ref in enumerate((first_ref, second_ref)):
        for r in range(4):
            for h in range(2):
                bulk_ref[t, r, h] = ref[0, 2 * r + h]
        for c in range(2):
            for h in range(2):
                even = ref[0, 4 * c + h]
                odd = ref[0, 4 * c + 2 + h]
                even_ref[t, c, h] = jnp.where(low, even, odd)
                odd_ref[t, c, h] = jnp.where(low, odd, even)


def route(scal, received):
    block = (1, 8, 8, HALF)
    return pl.pallas_call(
        route_kernel,
        grid_spec=pltpu.PrefetchScalarGridSpec(
            num_scalar_prefetch=1,
            grid=(1,),
            in_specs=[
                pl.BlockSpec(block, lambda _, s: (s[0] % N_COL, 0, 0, 0)),
                pl.BlockSpec(block, lambda _, s: ((s[0] + 1) % N_COL, 0, 0, 0)),
            ],
            out_specs=[VMEM, VMEM, VMEM],
        ),
        out_shape=[
            jax.ShapeDtypeStruct((2, 4, 2, 8, HALF), f32),
            jax.ShapeDtypeStruct((2, 2, 2, 8, HALF), f32),
            jax.ShapeDtypeStruct((2, 2, 2, 8, HALF), f32),
        ],
    )(scal, received, received)


def cols_kernel(scal, first_ref, second_ref, out_ref):
    low = scal[2] < N_ROW
    first, second = first_ref[...], second_ref[...]
    out_ref[0] = jnp.where(low, first, second)
    out_ref[1] = jnp.where(low, second, first)


def order_cols(scal, first, second):
    return pl.pallas_call(
        cols_kernel,
        in_specs=[SMEM, VMEM, VMEM],
        out_specs=VMEM,
        out_shape=jax.ShapeDtypeStruct((2, 2, 2, 2, 8, HALF), f32),
    )(scal, first, second)


def factor_half(block):
    groups = HALF // 8
    sub = lax.broadcasted_iota(jnp.int32, (8, HALF), 0)
    lane = lax.broadcasted_iota(jnp.int32, (8, HALF), 1)
    up = [block[8 * g : 8 * g + 8, :] for g in range(groups)]
    inv = [jnp.where(lane == sub + 8 * g, 1.0, 0.0).astype(f32) for g in range(groups)]
    upper, lower_inv = [], []

    def row(x, j):
        return jnp.broadcast_to(x[j : j + 1, :], (8, HALF))

    def column(x, c):
        return jnp.broadcast_to(x[:, c : c + 1], (8, HALF))

    for b in range(groups):
        rows, irows = up[b], inv[b]
        cols = [column(rows, 8 * b + j) for j in range(8)]
        diag = jnp.zeros((8, HALF), f32)
        for j in range(8):
            pivot = row(cols[j], j)
            recip = 1.0 / pivot
            diag = jnp.where(sub == j, pivot, diag)
            if j < 7:
                mult = jnp.where(sub > j, cols[j] * recip, 0.0)
                for l in range(j + 1, 8):
                    cols[l] = cols[l] - mult * row(cols[l], j)
                rows = rows - mult * row(rows, j)
                irows = irows - mult * row(irows, j)
        scale = lax.rsqrt(diag)
        rows = rows * scale
        irows = irows * scale
        upper.append(jnp.where(lane >= sub + 8 * b, rows, 0.0))
        lower_inv.append(irows)
        if b + 1 < groups:
            row_each = [row(rows, j) for j in range(8)]
            irow_each = [row(irows, j) for j in range(8)]
            flipped = rows.T
            for g in range(b + 1, groups):
                part = flipped[8 * g : 8 * g + 8, :]
                for j in range(8):
                    m = column(part, j)
                    up[g] = up[g] - m * row_each[j]
                    inv[g] = inv[g] - m * irow_each[j]
    return jnp.concatenate(upper, 0), jnp.concatenate(lower_inv, 0)


def factor_kernel(scal, lev, d_ref, out_hbm, out_ref, s_ref, u_ref, v_ref, sems):
    k = scal[0]

    def send(n):
        return pltpu.make_async_copy(out_ref.at[n], out_hbm.at[n], sems.at[n])

    def tile(n):
        return jnp.concatenate([d_ref[:, 2 * n + h].reshape(B, HALF) for h in range(2)], axis=1)

    s_ref[...] = tile(0)

    def step(t, _):
        def half(h, _):
            at = pl.ds(pl.multiple_of(h * HALF, HALF), HALF)
            u, v = factor_half(s_ref[at, at])
            u_ref[h] = u
            v_ref[h] = v

            @pl.when(h == 0)
            def _():
                l21 = dot_nt(s_ref[HALF:, 0:HALF], v)
                s_ref[HALF:, 0:HALF] = l21
                s_ref[HALF:, HALF:] = s_ref[HALF:, HALF:] - dot_nt(l21, l21)

            return 0

        lax.fori_loop(0, 2, half, 0)
        l21 = s_ref[HALF:, 0:HALF]
        zero = jnp.zeros((HALF, HALF), f32)
        v0, v1 = v_ref[0], v_ref[1]
        out_ref[t, 0:HALF, 0:HALF] = u_ref[0].T
        out_ref[t, 0:HALF, HALF:] = zero
        out_ref[t, HALF:, 0:HALF] = l21
        out_ref[t, HALF:, HALF:] = u_ref[1].T
        out_ref[2 + t, 0:HALF, 0:HALF] = v0
        out_ref[2 + t, 0:HALF, HALF:] = zero
        out_ref[2 + t, HALF:, 0:HALF] = -dot_nn(v1, dot_nn(l21, v0))
        out_ref[2 + t, HALF:, HALF:] = v1

        @pl.when(t == 0)
        def _():
            below = k + 1
            solved = by_level(dot_nt(tile(1), out_ref[2]), lev[below % N_ROW, below // N_ROW])
            out_ref[4] = solved
            s_ref[...] = tile(2) - dot_nt(solved, solved)
            for n in (0, 2, 4):
                send(n).start()

        return 0

    lax.fori_loop(0, 2, step, 0)
    for n in (1, 3):
        send(n).start()
    for n in range(5):
        send(n).wait()


def factor_two(scal, lev, diag):
    return pl.pallas_call(
        factor_kernel,
        in_specs=[SMEM, SMEM, VMEM],
        out_specs=HBM,
        out_shape=jax.ShapeDtypeStruct((5, B, B), f32),
        scratch_shapes=[
            pltpu.VMEM((5, B, B), f32),
            pltpu.VMEM((B, B), f32),
            pltpu.VMEM((2, HALF, HALF), f32),
            pltpu.VMEM((2, HALF, HALF), f32),
            pltpu.SemaphoreType.DMA((5,)),
        ],
        compiler_params=pltpu.CompilerParams(vmem_limit_bytes=8 << 20),
        cost_estimate=pl.CostEstimate(flops=3 * 10**10, bytes_accessed=10**6, transcendentals=0),
    )(scal, lev, diag)


def update_kernel(
    scal,
    lev,
    prec,
    rows_hbm,
    cols_hbm,
    f_hbm,
    mat_hbm,
    out_hbm,
    rows_ref,
    cols_ref,
    f_ref,
    mat_ref,
    out_ref,
    panel,
    sems,
    out_sems,
):
    k, p, q = scal[0], scal[1], scal[2]
    pairs = ((cols_hbm, cols_ref), (rows_hbm, rows_ref), (f_hbm, f_ref), (mat_hbm, mat_ref))
    fetches = [pltpu.make_async_copy(a, b, sems.at[n]) for n, (a, b) in enumerate(pairs)]
    for fetch in fetches:
        fetch.start()

    def store(r):
        at = pl.ds(pl.multiple_of(r * 1024, 1024), 1024)
        return pltpu.make_async_copy(out_ref.at[at], out_hbm.at[at], out_sems.at[r])

    def level_of(t, i):
        return lev[i % N_ROW, 4 * t + i // N_ROW]

    fetches[0].wait()
    fetches[1].wait()
    for t in range(2):
        for h in range(2):
            lanes = slice(h * HALF, (h + 1) * HALF)
            for r in range(4):
                for x in range(4):
                    for z in range(8):
                        at = 8 * (4 * z + x)
                        panel[t, r, at : at + 8, lanes] = rows_ref[x, z, t, r, h]
            for c in range(2):
                for part in range(2):
                    at = slice(part * HALF, (part + 1) * HALF)
                    panel[t, 4 + c, at, lanes] = cols_ref[:, part, t, c, h].reshape(HALF, HALF)
    fetches[2].wait()

    def solve(n, _):
        i = jnp.where(n < 4, n * N_ROW + p, (n - 4) * N_COL + q)

        @pl.when(i > k)
        def _():
            panel[0, n] = by_level(dot_nt(panel[0, n], f_ref[2]), level_of(0, i))
            level = level_of(1, i)

            @pl.when((i > k + 1) & (level == 2))
            def _():
                raw = panel[1, n] - dot_nt(panel[0, n], f_ref[4])
                panel[1, n] = dot_nt(raw, f_ref[3])

            @pl.when((i > k + 1) & (level == 1))
            def _():
                raw = rounded(panel[1, n] - dot_narrow(panel[0, n], f_ref[4]))
                panel[1, n] = rounded(dot_nt(raw, f_ref[3]))

        return 0

    lax.fori_loop(0, 6, solve, 0)
    fetches[3].wait()

    def trail(n, _):
        r, c = n // 2, n % 2
        i = r * N_ROW + p
        j = c * N_COL + q
        level = prec[r, c]
        active = (i >= j) & (j > k)
        halves = [pl.ds(r * 1024 + c * 2 + h, B, stride=4) for h in range(2)]

        def put(value):
            for h in range(2):
                out_ref[halves[h], :] = value[:, h * HALF : (h + 1) * HALF]

        def get():
            return jnp.concatenate([mat_ref[halves[h], :] for h in range(2)], axis=1)

        own_first = (j == k) & (i > k)
        own_second = (j == k + 1) & (i > k + 1)
        diagonal = (i == j) & ((j == k) | (j == k + 1))
        plain = jnp.logical_not(own_first | own_second | diagonal)

        @pl.when(plain & (level == 2))
        def _():
            put(get())

            @pl.when(active)
            def _():
                put(get() - dot_nt(panel[0, r], panel[0, 4 + c]) - dot_nt(panel[1, r], panel[1, 4 + c]))

        @pl.when(plain & (level == 1))
        def _():
            put(rounded(get()))

            @pl.when(active)
            def _():
                once = rounded(rounded(get()) - dot_narrow(panel[0, r], panel[0, 4 + c]))
                put(rounded(once - dot_narrow(panel[1, r], panel[1, 4 + c])))

        @pl.when(plain & (level == 0))
        def _():
            put(jnp.zeros((B, B), f32))

        @pl.when(own_first)
        def _():
            put(panel[0, r])

        @pl.when(own_second)
        def _():
            put(panel[1, r])

        @pl.when(diagonal)
        def _():
            put(f_ref[j - k])

        @pl.when(c == 1)
        def _():
            store(r).start()

        return 0

    lax.fori_loop(0, 8, trail, 0)
    for r in range(4):
        store(r).wait()


def update(scal, lev, prec, row_tiles, col_tiles, factors, mat):
    operands = (row_tiles, col_tiles, factors, mat)
    return pl.pallas_call(
        update_kernel,
        in_specs=[SMEM, SMEM, SMEM] + [HBM] * 4,
        out_specs=HBM,
        out_shape=jax.ShapeDtypeStruct(mat.shape, f32),
        scratch_shapes=[pltpu.VMEM(x.shape, f32) for x in operands]
        + [
            pltpu.VMEM(mat.shape, f32),
            pltpu.VMEM((2, 6, B, B), f32),
            pltpu.SemaphoreType.DMA((4,)),
            pltpu.SemaphoreType.DMA((4,)),
        ],
        compiler_params=pltpu.CompilerParams(vmem_limit_bytes=20 << 20),
        cost_estimate=pl.CostEstimate(flops=10**10, bytes_accessed=10**7, transcendentals=0),
    )(scal, lev, prec, *operands)


def cross_pairs(odd):
    pairs = []
    for p in range(N_ROW):
        for q in range(N_COL):
            low = q < N_ROW
            first = low != odd
            row = q if low else q - N_ROW
            col = p if first else p + N_ROW
            pairs.append((p * N_COL + q, row * N_COL + col))
    return pairs


def per_device(matrix, precision, first_col):
    p = lax.axis_index("row")
    q = lax.axis_index("col")
    k = first_col[0]
    scal = jnp.stack([k, p, q]).astype(jnp.int32)
    prec = precision.reshape(4, 2)
    mat = matrix.reshape(4096, HALF)

    z_groups = [[4 * z + x for z in range(8)] for x in range(4)]
    x_groups = [[4 * z + x for x in range(4)] for z in range(8)]

    sent_diag, sent_bulk = pack(scal, prec, mat)
    got_diag = lax.all_to_all(sent_diag, "col", 0, 0)
    seen = lax.all_gather(diag_parts(scal, got_diag), "row")
    got_bulk = lax.all_to_all(sent_bulk, "col", 0, 0)
    bulk, even, odd = route(scal, got_bulk)
    diags = lax.all_to_all(diag_copies(scal, seen), "col", 0, 0)
    lev = seen[:, 4, :, 0].astype(jnp.int32)

    both = ("row", "col")
    first = lax.ppermute(even, both, cross_pairs(False))
    second = lax.ppermute(odd, both, cross_pairs(True))
    col_tiles = lax.all_gather(order_cols(scal, first, second), "row")
    slab = lax.all_gather(bulk, "col", axis_index_groups=z_groups)
    diags, slab = lax.optimization_barrier((diags, slab))

    row_tiles = lax.all_to_all(
        jnp.broadcast_to(slab[None], (4,) + slab.shape), "col", 0, 0, axis_index_groups=x_groups
    )
    factors = factor_two(scal, lev, diags)
    out = update(scal, lev, prec, row_tiles, col_tiles, factors, mat)
    return out.reshape(matrix.shape)


def solution(mesh):
    in_specs = (P(None, "row", None, None, "col", None), P(None, "row", None, "col"), P())
    out_specs = P(None, "row", None, None, "col", None)
    return jax.shard_map(
        per_device, mesh=mesh, in_specs=in_specs, out_specs=out_specs, check_vma=False
    )
```

```python
import functools

import jax
import jax.numpy as jnp
from jax import lax
from jax.experimental import pallas as pl
from jax.experimental.pallas import tpu as pltpu
from jax.sharding import PartitionSpec as P

HIGHEST = lax.Precision.HIGHEST
f32 = jnp.float32
N_ROW = 16
N_COL = 32
B = 256
HALF = 128
SMEM = pl.BlockSpec(memory_space=pltpu.SMEM)
VMEM = pl.BlockSpec(memory_space=pltpu.VMEM)
HBM = pl.BlockSpec(memory_space=pltpu.HBM)


def dot_nt(a, b):
    return lax.dot_general(
        a, b, (((1,), (1,)), ((), ())), precision=HIGHEST, preferred_element_type=f32
    )


def dot_nn(a, b):
    return lax.dot_general(
        a, b, (((1,), (0,)), ((), ())), precision=HIGHEST, preferred_element_type=f32
    )


def dot_narrow(a, b):
    return lax.dot_general(
        a.astype(jnp.bfloat16),
        b.astype(jnp.bfloat16),
        (((1,), (1,)), ((), ())),
        preferred_element_type=f32,
    )


def rounded(x):
    return x.astype(jnp.bfloat16).astype(f32)


def by_level(x, level):
    return jnp.where(level == 2, x, jnp.where(level == 1, rounded(x), 0.0))


def pack_kernel(r0, scal, prec, mat_ref, diag_ref, bulk_ref):
    k, p, q = scal[0], scal[1], scal[2]
    col = jnp.where(q == k % N_COL, k // N_COL, (k + 1) // N_COL)
    here_r = jnp.where(p == k % N_ROW, k // N_ROW, (k + 1) // N_ROW)
    sub = lax.broadcasted_iota(jnp.int32, (8, HALF), 0)
    levels = jnp.zeros((8, HALF), f32)
    for r in range(4):
        level = prec[r, col]
        levels = jnp.where(sub % 4 == r, level.astype(f32), levels)
    diag_ref[:, 2] = jnp.broadcast_to(levels[None], (32, 8, HALF))
    for r in range(r0, 4):
        for h in range(2):
            rows = mat_ref[pl.ds(r * 1024 + col * 2 + h, B, stride=4), :]
            rows = by_level(rows, prec[r, col]).reshape(32, 8, HALF)
            bulk_ref[:, (r - r0) * 2 + h] = rows

            @pl.when(here_r == r)
            def _():
                diag_ref[:, h] = rows


def pack(r0, scal, prec, mat):
    return pl.pallas_call(
        functools.partial(pack_kernel, r0),
        in_specs=[SMEM, SMEM, VMEM],
        out_specs=[VMEM, VMEM],
        out_shape=[
            jax.ShapeDtypeStruct((N_COL, 3, 8, HALF), f32),
            jax.ShapeDtypeStruct((N_COL, 8 - 2 * r0, 8, HALF), f32),
        ],
        compiler_params=pltpu.CompilerParams(vmem_limit_bytes=8 << 20),
    )(scal, prec, mat)


def diag_kernel(scal, first_ref, second_ref, out_ref):
    k, p = scal[0], scal[1]
    sub = lax.broadcasted_iota(jnp.int32, (8, HALF), 0)
    out_ref[0:2] = first_ref[0, 0:2]
    out_ref[2:4] = second_ref[0, 0:2]
    out_ref[4] = jnp.where(sub < 4, first_ref[0, 2], second_ref[0, 2])


def diag_parts(scal, received):
    block = (1, 3, 8, HALF)
    return pl.pallas_call(
        diag_kernel,
        grid_spec=pltpu.PrefetchScalarGridSpec(
            num_scalar_prefetch=1,
            grid=(1,),
            in_specs=[
                pl.BlockSpec(block, lambda _, s: (s[0] % N_COL, 0, 0, 0)),
                pl.BlockSpec(block, lambda _, s: ((s[0] + 1) % N_COL, 0, 0, 0)),
            ],
            out_specs=VMEM,
        ),
        out_shape=jax.ShapeDtypeStruct((5, 8, HALF), f32),
    )(scal, received, received)


def route_kernel(r0, c0, scal, first_ref, second_ref, here_ref, below_ref, line_ref, even_ref, odd_ref):
    low = scal[2] < N_ROW
    rows = 4 - r0
    for z in range(8):
        for t, ref in enumerate((first_ref, second_ref)):
            line_ref[z, 2 * rows * t : 2 * rows * (t + 1)] = ref[0]
        line_ref[z, 4 * rows : 4 * rows + 2] = here_ref[0, 0:2]
        line_ref[z, 4 * rows + 2 : 4 * rows + 6] = below_ref[0, 0:4]
    for t, ref in enumerate((first_ref, second_ref)):
        for c in range(c0, 2):
            for h in range(2):
                even = ref[0, 2 * max(2 * c - r0, 0) + h]
                odd = ref[0, 2 * (2 * c + 1 - r0) + h]
                even_ref[t, c - c0, h] = jnp.where(low, even, odd)
                odd_ref[t, c - c0, h] = jnp.where(low, odd, even)


def route(r0, c0, scal, received, seen):
    block = (1, 8 - 2 * r0, 8, HALF)
    part = (1, 5, 8, HALF)
    cross = jax.ShapeDtypeStruct((2, 2 - c0, 2, 8, HALF), f32)
    return pl.pallas_call(
        functools.partial(route_kernel, r0, c0),
        grid_spec=pltpu.PrefetchScalarGridSpec(
            num_scalar_prefetch=1,
            grid=(1,),
            in_specs=[
                pl.BlockSpec(block, lambda _, s: (s[0] % N_COL, 0, 0, 0)),
                pl.BlockSpec(block, lambda _, s: ((s[0] + 1) % N_COL, 0, 0, 0)),
                pl.BlockSpec(part, lambda _, s: (s[0] % N_ROW, 0, 0, 0)),
                pl.BlockSpec(part, lambda _, s: ((s[0] + 1) % N_ROW, 0, 0, 0)),
            ],
            out_specs=[VMEM, VMEM, VMEM],
        ),
        out_shape=[jax.ShapeDtypeStruct((8, 22 - 4 * r0, 8, HALF), f32), cross, cross],
    )(scal, received, received, seen, seen)


def cols_kernel(scal, first_ref, second_ref, out_ref):
    low = scal[2] < N_ROW
    first, second = first_ref[...], second_ref[...]
    for y in range(8):
        out_ref[y, 0] = jnp.where(low, first, second)
        out_ref[y, 1] = jnp.where(low, second, first)


def col_copies(scal, first, second):
    return pl.pallas_call(
        cols_kernel,
        in_specs=[SMEM, VMEM, VMEM],
        out_specs=VMEM,
        out_shape=jax.ShapeDtypeStruct((8, 2) + first.shape, f32),
    )(scal, first, second)


def factor_half(block):
    groups = HALF // 8
    sub = lax.broadcasted_iota(jnp.int32, (8, HALF), 0)
    lane = lax.broadcasted_iota(jnp.int32, (8, HALF), 1)
    up = [block[8 * g : 8 * g + 8, :] for g in range(groups)]
    inv = [jnp.where(lane == sub + 8 * g, 1.0, 0.0).astype(f32) for g in range(groups)]
    upper, lower_inv = [], []

    def row(x, j):
        return jnp.broadcast_to(x[j : j + 1, :], (8, HALF))

    def column(x, c):
        return jnp.broadcast_to(x[:, c : c + 1], (8, HALF))

    for b in range(groups):
        rows, irows = up[b], inv[b]
        cols = [column(rows, 8 * b + j) for j in range(8)]
        diag = jnp.zeros((8, HALF), f32)
        for j in range(8):
            pivot = row(cols[j], j)
            recip = 1.0 / pivot
            diag = jnp.where(sub == j, pivot, diag)
            if j < 7:
                mult = jnp.where(sub > j, cols[j] * recip, 0.0)
                for l in range(j + 1, 8):
                    cols[l] = cols[l] - mult * row(cols[l], j)
                rows = rows - mult * row(rows, j)
                irows = irows - mult * row(irows, j)
        scale = lax.rsqrt(diag)
        rows = rows * scale
        irows = irows * scale
        upper.append(jnp.where(lane >= sub + 8 * b, rows, 0.0))
        lower_inv.append(irows)
        if b + 1 < groups:
            row_each = [row(rows, j) for j in range(8)]
            irow_each = [row(irows, j) for j in range(8)]
            flipped = rows.T
            for g in range(b + 1, groups):
                part = flipped[8 * g : 8 * g + 8, :]
                for j in range(8):
                    m = column(part, j)
                    up[g] = up[g] - m * row_each[j]
                    inv[g] = inv[g] - m * irow_each[j]
    return jnp.concatenate(upper, 0), jnp.concatenate(lower_inv, 0)


def factor_tile(out_ref, s_ref, u_ref, v_ref):
    def half(h, _):
        at = pl.ds(pl.multiple_of(h * HALF, HALF), HALF)
        u, v = factor_half(s_ref[at, at])
        u_ref[h] = u
        v_ref[h] = v

        @pl.when(h == 0)
        def _():
            l21 = dot_nt(s_ref[HALF:, 0:HALF], v)
            s_ref[HALF:, 0:HALF] = l21
            s_ref[HALF:, HALF:] = s_ref[HALF:, HALF:] - dot_nt(l21, l21)

        return 0

    lax.fori_loop(0, 2, half, 0)
    l21 = s_ref[HALF:, 0:HALF]
    zero = jnp.zeros((HALF, HALF), f32)
    v0, v1 = v_ref[0], v_ref[1]
    out_ref[0, 0:HALF, 0:HALF] = u_ref[0].T
    out_ref[0, 0:HALF, HALF:] = zero
    out_ref[0, HALF:, 0:HALF] = l21
    out_ref[0, HALF:, HALF:] = u_ref[1].T
    out_ref[1, 0:HALF, 0:HALF] = v0
    out_ref[1, 0:HALF, HALF:] = zero
    out_ref[1, HALF:, 0:HALF] = -dot_nn(v1, dot_nn(l21, v0))
    out_ref[1, HALF:, HALF:] = v1


FACTOR_SCRATCH = [
    pltpu.VMEM((B, B), f32),
    pltpu.VMEM((2, HALF, HALF), f32),
    pltpu.VMEM((2, HALF, HALF), f32),
]


def first_kernel(scal, lev, d_ref, out_ref, d_rows, s_ref, u_ref, v_ref):
    below = scal[0] + 1
    for x in range(4):
        for z in range(8):
            d_rows[4 * z + x] = d_ref[x, z]

    def tile(n):
        return jnp.concatenate([d_rows[:, 2 * n + h].reshape(B, HALF) for h in range(2)], axis=1)

    s_ref[...] = tile(0)
    factor_tile(out_ref, s_ref, u_ref, v_ref)
    solved = by_level(dot_nt(tile(1), out_ref[1]), lev[below % N_ROW, below // N_ROW])
    out_ref[2] = solved
    out_ref[3] = tile(2) - dot_nt(solved, solved)


def factor_first(scal, lev, diags):
    return pl.pallas_call(
        first_kernel,
        in_specs=[SMEM, SMEM, VMEM],
        out_specs=VMEM,
        out_shape=jax.ShapeDtypeStruct((4, B, B), f32),
        scratch_shapes=[pltpu.VMEM((N_COL, 6, 8, HALF), f32)] + FACTOR_SCRATCH,
        compiler_params=pltpu.CompilerParams(vmem_limit_bytes=8 << 20),
        cost_estimate=pl.CostEstimate(flops=15 * 10**9, bytes_accessed=10**6, transcendentals=0),
    )(scal, lev, diags)


def second_kernel(tile_hbm, out_ref, s_ref, u_ref, v_ref, sem):
    fetch = pltpu.make_async_copy(tile_hbm.at[3], s_ref, sem)
    fetch.start()
    fetch.wait()
    factor_tile(out_ref, s_ref, u_ref, v_ref)


def factor_second(tiles):
    return pl.pallas_call(
        second_kernel,
        in_specs=[HBM],
        out_specs=VMEM,
        out_shape=jax.ShapeDtypeStruct((2, B, B), f32),
        scratch_shapes=FACTOR_SCRATCH + [pltpu.SemaphoreType.DMA(())],
        compiler_params=pltpu.CompilerParams(vmem_limit_bytes=8 << 20),
        cost_estimate=pl.CostEstimate(flops=15 * 10**9, bytes_accessed=10**6, transcendentals=0),
    )(tiles)


def update_kernel(
    r0,
    c0,
    scal,
    lev,
    prec,
    own_hbm,
    other_hbm,
    f_hbm,
    g_hbm,
    mat_hbm,
    rows_hbm,
    out_hbm,
    own_ref,
    other_ref,
    f_ref,
    g_ref,
    mat_ref,
    rows_ref,
    out_ref,
    panel,
    sems,
    out_sems,
):
    k, p, q = scal[0], scal[1], scal[2]
    core = p % 2
    rows = 4 - r0
    tiles = rows + 2 - c0
    pairs = (
        (own_hbm, own_ref),
        (other_hbm, other_ref),
        (rows_hbm, rows_ref),
        (f_hbm, f_ref),
        (g_hbm, g_ref),
        (mat_hbm, mat_ref),
    )
    fetches = [pltpu.make_async_copy(a, b, sems.at[n]) for n, (a, b) in enumerate(pairs)]
    for fetch in fetches:
        fetch.start()

    def store(r):
        at = pl.ds(pl.multiple_of(r * 1024, 1024), 1024)
        return pltpu.make_async_copy(out_ref.at[at], out_hbm.at[at], out_sems.at[r])

    def level_of(t, i):
        return lev[i % N_ROW, 4 * t + i // N_ROW]

    for fetch in fetches[:3]:
        fetch.wait()
    for t in range(2):
        for h in range(2):
            lanes = slice(h * HALF, (h + 1) * HALF)
            for c in range(2 - c0):
                for part in range(2):
                    for y in range(8):
                        at = 8 * (16 * part + 2 * y)
                        for ref, side in ((own_ref, core), (other_ref, 1 - core)):
                            to = pl.ds(pl.multiple_of(at + 8 * side, 8), 8)
                            panel[t, rows + c, to, lanes] = ref[y, part, t, c, h]
            for r in range(rows):
                for x in range(4):
                    for z in range(8):
                        at = 8 * (4 * z + x)
                        panel[t, r, at : at + 8, lanes] = rows_ref[x, z, 2 * rows * t + 2 * r + h]
    fetches[3].wait()
    fetches[4].wait()

    def solve(n, _):
        i = jnp.where(n < rows, (n + r0) * N_ROW + p, (n - rows + c0) * N_COL + q)

        @pl.when(i > k)
        def _():
            panel[0, n] = by_level(dot_nt(panel[0, n], f_ref[1]), level_of(0, i))
            level = level_of(1, i)

            @pl.when((i > k + 1) & (level == 2))
            def _():
                raw = panel[1, n] - dot_nt(panel[0, n], f_ref[2])
                panel[1, n] = dot_nt(raw, g_ref[1])

            @pl.when((i > k + 1) & (level == 1))
            def _():
                raw = rounded(panel[1, n] - dot_narrow(panel[0, n], f_ref[2]))
                panel[1, n] = rounded(dot_nt(raw, g_ref[1]))

        return 0

    lax.fori_loop(0, tiles, solve, 0)
    fetches[5].wait()

    def trail(n, _):
        r, c = n // 2, n % 2
        i = r * N_ROW + p
        j = c * N_COL + q
        level = prec[r, c]
        active = (i >= j) & (j > k)
        row_at = jnp.maximum(r - r0, 0)
        col_at = rows + jnp.maximum(c - c0, 0)
        halves = [pl.ds(r * 1024 + c * 2 + h, B, stride=4) for h in range(2)]

        def put(value):
            for h in range(2):
                out_ref[halves[h], :] = value[:, h * HALF : (h + 1) * HALF]

        def get():
            return jnp.concatenate([mat_ref[halves[h], :] for h in range(2)], axis=1)

        own_first = (j == k) & (i > k)
        own_second = (j == k + 1) & (i > k + 1)
        diagonal = (i == j) & ((j == k) | (j == k + 1))
        plain = jnp.logical_not(own_first | own_second | diagonal)

        @pl.when(plain & (level == 2))
        def _():
            put(get())

            @pl.when(active)
            def _():
                put(get() - dot_nt(panel[0, row_at], panel[0, col_at]) - dot_nt(panel[1, row_at], panel[1, col_at]))

        @pl.when(plain & (level == 1))
        def _():
            put(rounded(get()))

            @pl.when(active)
            def _():
                once = rounded(rounded(get()) - dot_narrow(panel[0, row_at], panel[0, col_at]))
                put(rounded(once - dot_narrow(panel[1, row_at], panel[1, col_at])))

        @pl.when(plain & (level == 0))
        def _():
            put(jnp.zeros((B, B), f32))

        @pl.when(own_first)
        def _():
            put(panel[0, row_at])

        @pl.when(own_second)
        def _():
            put(panel[1, row_at])

        @pl.when(diagonal & (j == k))
        def _():
            put(f_ref[0])

        @pl.when(diagonal & (j == k + 1))
        def _():
            put(g_ref[0])

        @pl.when(c == 1)
        def _():
            store(r).start()

        return 0

    lax.fori_loop(0, 8, trail, 0)
    for r in range(4):
        store(r).wait()


def update(r0, c0, scal, lev, prec, *operands):
    mat = operands[4]
    return pl.pallas_call(
        functools.partial(update_kernel, r0, c0),
        in_specs=[SMEM, SMEM, SMEM] + [HBM] * 6,
        out_specs=HBM,
        out_shape=jax.ShapeDtypeStruct(mat.shape, f32),
        scratch_shapes=[pltpu.VMEM(x.shape, f32) for x in operands]
        + [
            pltpu.VMEM(mat.shape, f32),
            pltpu.VMEM((2, 6 - r0 - c0, B, B), f32),
            pltpu.SemaphoreType.DMA((6,)),
            pltpu.SemaphoreType.DMA((4,)),
        ],
        compiler_params=pltpu.CompilerParams(vmem_limit_bytes=20 << 20),
        cost_estimate=pl.CostEstimate(flops=10**10, bytes_accessed=10**7, transcendentals=0),
    )(scal, lev, prec, *operands)


def cross_pairs(odd):
    pairs = []
    for p in range(N_ROW):
        for q in range(N_COL):
            low = q < N_ROW
            first = low != odd
            row = q if low else q - N_ROW
            col = p if first else p + N_ROW
            pairs.append((p * N_COL + q, row * N_COL + col))
    return pairs


def two_steps(r0, c0, scal, prec, mat):
    both = ("row", "col")
    z_groups = [[4 * z + x for z in range(8)] for x in range(4)]
    x_groups = [[4 * z + x for x in range(4)] for z in range(8)]
    y_groups = [[2 * y + c for y in range(8)] for c in range(2)]
    split = 16 - 4 * r0

    sent_diag, sent_bulk = pack(r0, scal, prec, mat)
    got_diag = lax.all_to_all(sent_diag, "col", 0, 0)
    seen = lax.all_gather(diag_parts(scal, got_diag), "row")
    got_bulk = lax.all_to_all(sent_bulk, "col", 0, 0)
    lev = seen[:, 4, :, 0].astype(jnp.int32)

    line, even, odd = route(r0, c0, scal, got_bulk, seen)
    line = lax.all_to_all(line, "col", 0, 0, axis_index_groups=z_groups)
    first = lax.ppermute(even, both, cross_pairs(False))
    second = lax.ppermute(odd, both, cross_pairs(True))

    diag_line = jnp.broadcast_to(line[None, :, split:], (4, 8, 6, 8, HALF))
    diags = lax.all_to_all(diag_line, "col", 0, 0, axis_index_groups=x_groups)
    copies = col_copies(scal, first, second)
    diags, copies = lax.optimization_barrier((diags, copies))

    own_cols = lax.all_to_all(copies, "row", 0, 0, axis_index_groups=y_groups)
    factors = factor_first(scal, lev, diags)
    own_cols, factors, line = lax.optimization_barrier((own_cols, factors, line))

    other_cols = lax.ppermute(own_cols, "row", [(i, i ^ 1) for i in range(N_ROW)])
    bulk_line = jnp.broadcast_to(line[None, :, :split], (4, 8, split, 8, HALF))
    row_tiles = lax.all_to_all(bulk_line, "col", 0, 0, axis_index_groups=x_groups)
    seconds = factor_second(factors)
    return update(
        r0, c0, scal, lev, prec, own_cols, other_cols, factors, seconds, mat, row_tiles
    )


def per_device(matrix, precision, first_col):
    p = lax.axis_index("row")
    q = lax.axis_index("col")
    k = first_col[0]
    scal = jnp.stack([k, p, q]).astype(jnp.int32)
    prec = precision.reshape(4, 2)
    mat = matrix.reshape(4096, HALF)
    out = two_steps(0, 0, scal, prec, mat)
    return out.reshape(matrix.shape)


def solution(mesh):
    in_specs = (P(None, "row", None, None, "col", None), P(None, "row", None, "col"), P())
    out_specs = P(None, "row", None, None, "col", None)
    return jax.shard_map(
        per_device, mesh=mesh, in_specs=in_specs, out_specs=out_specs, check_vma=False
    )
```

```python
import functools

import jax
import jax.numpy as jnp
from jax import lax
from jax.experimental import pallas as pl
from jax.experimental.pallas import tpu as pltpu
from jax.sharding import PartitionSpec as P

HIGHEST = lax.Precision.HIGHEST
f32 = jnp.float32
N_ROW = 16
N_COL = 32
B = 256
HALF = 128
SMEM = pl.BlockSpec(memory_space=pltpu.SMEM)
VMEM = pl.BlockSpec(memory_space=pltpu.VMEM)
HBM = pl.BlockSpec(memory_space=pltpu.HBM)


def dot_nt(a, b):
    return lax.dot_general(
        a, b, (((1,), (1,)), ((), ())), precision=HIGHEST, preferred_element_type=f32
    )


def dot_nn(a, b):
    return lax.dot_general(
        a, b, (((1,), (0,)), ((), ())), precision=HIGHEST, preferred_element_type=f32
    )


def dot_narrow(a, b):
    return lax.dot_general(
        a.astype(jnp.bfloat16),
        b.astype(jnp.bfloat16),
        (((1,), (1,)), ((), ())),
        preferred_element_type=f32,
    )


def rounded(x):
    return x.astype(jnp.bfloat16).astype(f32)


def by_level(x, level):
    return jnp.where(level == 2, x, jnp.where(level == 1, rounded(x), 0.0))


def pack_kernel(r0, scal, prec, mat_ref, diag_ref, bulk_ref):
    k, p, q = scal[0], scal[1], scal[2]
    col = jnp.where(q == k % N_COL, k // N_COL, (k + 1) // N_COL)
    here_r = jnp.where(p == k % N_ROW, k // N_ROW, (k + 1) // N_ROW)
    sub = lax.broadcasted_iota(jnp.int32, (8, HALF), 0)
    levels = jnp.zeros((8, HALF), f32)
    for r in range(4):
        level = prec[r, col]
        levels = jnp.where(sub % 4 == r, level.astype(f32), levels)
    diag_ref[:, 2] = jnp.broadcast_to(levels[None], (32, 8, HALF))
    for r in range(r0, 4):
        for h in range(2):
            rows = mat_ref[pl.ds(r * 1024 + col * 2 + h, B, stride=4), :]
            rows = by_level(rows, prec[r, col]).reshape(32, 8, HALF)
            bulk_ref[:, (r - r0) * 2 + h] = rows

            @pl.when(here_r == r)
            def _():
                diag_ref[:, h] = rows


def pack(r0, scal, prec, mat):
    return pl.pallas_call(
        functools.partial(pack_kernel, r0),
        in_specs=[SMEM, SMEM, VMEM],
        out_specs=[VMEM, VMEM],
        out_shape=[
            jax.ShapeDtypeStruct((N_COL, 3, 8, HALF), f32),
            jax.ShapeDtypeStruct((N_COL, 8 - 2 * r0, 8, HALF), f32),
        ],
        compiler_params=pltpu.CompilerParams(vmem_limit_bytes=8 << 20),
    )(scal, prec, mat)


def diag_kernel(scal, first_ref, second_ref, out_ref):
    k, p = scal[0], scal[1]
    sub = lax.broadcasted_iota(jnp.int32, (8, HALF), 0)
    out_ref[0:2] = first_ref[0, 0:2]
    out_ref[2:4] = second_ref[0, 0:2]
    out_ref[4] = jnp.where(sub < 4, first_ref[0, 2], second_ref[0, 2])


def diag_parts(scal, received):
    block = (1, 3, 8, HALF)
    return pl.pallas_call(
        diag_kernel,
        grid_spec=pltpu.PrefetchScalarGridSpec(
            num_scalar_prefetch=1,
            grid=(1,),
            in_specs=[
                pl.BlockSpec(block, lambda _, s: (s[0] % N_COL, 0, 0, 0)),
                pl.BlockSpec(block, lambda _, s: ((s[0] + 1) % N_COL, 0, 0, 0)),
            ],
            out_specs=VMEM,
        ),
        out_shape=jax.ShapeDtypeStruct((5, 8, HALF), f32),
    )(scal, received, received)


def route_kernel(r0, c0, scal, first_ref, second_ref, here_ref, below_ref, line_ref, even_ref, odd_ref):
    low = scal[2] < N_ROW
    rows = 4 - r0
    for z in range(8):
        for t, ref in enumerate((first_ref, second_ref)):
            line_ref[z, 2 * rows * t : 2 * rows * (t + 1)] = ref[0]
        line_ref[z, 4 * rows : 4 * rows + 2] = here_ref[0, 0:2]
        line_ref[z, 4 * rows + 2 : 4 * rows + 6] = below_ref[0, 0:4]
    for t, ref in enumerate((first_ref, second_ref)):
        for c in range(c0, 2):
            for h in range(2):
                even = ref[0, 2 * max(2 * c - r0, 0) + h]
                odd = ref[0, 2 * (2 * c + 1 - r0) + h]
                even_ref[t, c - c0, h] = jnp.where(low, even, odd)
                odd_ref[t, c - c0, h] = jnp.where(low, odd, even)


def route(r0, c0, scal, received, seen):
    block = (1, 8 - 2 * r0, 8, HALF)
    part = (1, 5, 8, HALF)
    cross = jax.ShapeDtypeStruct((2, 2 - c0, 2, 8, HALF), f32)
    return pl.pallas_call(
        functools.partial(route_kernel, r0, c0),
        grid_spec=pltpu.PrefetchScalarGridSpec(
            num_scalar_prefetch=1,
            grid=(1,),
            in_specs=[
                pl.BlockSpec(block, lambda _, s: (s[0] % N_COL, 0, 0, 0)),
                pl.BlockSpec(block, lambda _, s: ((s[0] + 1) % N_COL, 0, 0, 0)),
                pl.BlockSpec(part, lambda _, s: (s[0] % N_ROW, 0, 0, 0)),
                pl.BlockSpec(part, lambda _, s: ((s[0] + 1) % N_ROW, 0, 0, 0)),
            ],
            out_specs=[VMEM, VMEM, VMEM],
        ),
        out_shape=[jax.ShapeDtypeStruct((8, 22 - 4 * r0, 8, HALF), f32), cross, cross],
    )(scal, received, received, seen, seen)


def cols_kernel(scal, first_ref, second_ref, out_ref):
    low = scal[2] < N_ROW
    first, second = first_ref[...], second_ref[...]
    out_ref[0] = jnp.where(low, first, second)
    out_ref[1] = jnp.where(low, second, first)


def order_cols(scal, first, second):
    return pl.pallas_call(
        cols_kernel,
        in_specs=[SMEM, VMEM, VMEM],
        out_specs=VMEM,
        out_shape=jax.ShapeDtypeStruct((2,) + first.shape, f32),
    )(scal, first, second)


def factor_half(block):
    groups = HALF // 8
    sub = lax.broadcasted_iota(jnp.int32, (8, HALF), 0)
    lane = lax.broadcasted_iota(jnp.int32, (8, HALF), 1)
    up = [block[8 * g : 8 * g + 8, :] for g in range(groups)]
    inv = [jnp.where(lane == sub + 8 * g, 1.0, 0.0).astype(f32) for g in range(groups)]
    upper, lower_inv = [], []

    def row(x, j):
        return jnp.broadcast_to(x[j : j + 1, :], (8, HALF))

    def column(x, c):
        return jnp.broadcast_to(x[:, c : c + 1], (8, HALF))

    for b in range(groups):
        rows, irows = up[b], inv[b]
        cols = [column(rows, 8 * b + j) for j in range(8)]
        diag = jnp.zeros((8, HALF), f32)
        for j in range(8):
            pivot = row(cols[j], j)
            recip = 1.0 / pivot
            diag = jnp.where(sub == j, pivot, diag)
            if j < 7:
                mult = jnp.where(sub > j, cols[j] * recip, 0.0)
                for l in range(j + 1, 8):
                    cols[l] = cols[l] - mult * row(cols[l], j)
                rows = rows - mult * row(rows, j)
                irows = irows - mult * row(irows, j)
        scale = lax.rsqrt(diag)
        rows = rows * scale
        irows = irows * scale
        upper.append(jnp.where(lane >= sub + 8 * b, rows, 0.0))
        lower_inv.append(irows)
        if b + 1 < groups:
            row_each = [row(rows, j) for j in range(8)]
            irow_each = [row(irows, j) for j in range(8)]
            flipped = rows.T
            for g in range(b + 1, groups):
                part = flipped[8 * g : 8 * g + 8, :]
                for j in range(8):
                    m = column(part, j)
                    up[g] = up[g] - m * row_each[j]
                    inv[g] = inv[g] - m * irow_each[j]
    return jnp.concatenate(upper, 0), jnp.concatenate(lower_inv, 0)


def factor_tile(out_ref, s_ref, u_ref, v_ref):
    def half(h, _):
        at = pl.ds(pl.multiple_of(h * HALF, HALF), HALF)
        u, v = factor_half(s_ref[at, at])
        u_ref[h] = u
        v_ref[h] = v

        @pl.when(h == 0)
        def _():
            l21 = dot_nt(s_ref[HALF:, 0:HALF], v)
            s_ref[HALF:, 0:HALF] = l21
            s_ref[HALF:, HALF:] = s_ref[HALF:, HALF:] - dot_nt(l21, l21)

        return 0

    lax.fori_loop(0, 2, half, 0)
    l21 = s_ref[HALF:, 0:HALF]
    zero = jnp.zeros((HALF, HALF), f32)
    v0, v1 = v_ref[0], v_ref[1]
    out_ref[0, 0:HALF, 0:HALF] = u_ref[0].T
    out_ref[0, 0:HALF, HALF:] = zero
    out_ref[0, HALF:, 0:HALF] = l21
    out_ref[0, HALF:, HALF:] = u_ref[1].T
    out_ref[1, 0:HALF, 0:HALF] = v0
    out_ref[1, 0:HALF, HALF:] = zero
    out_ref[1, HALF:, 0:HALF] = -dot_nn(v1, dot_nn(l21, v0))
    out_ref[1, HALF:, HALF:] = v1


def final_kernel(
    r0,
    c0,
    scal,
    lev,
    prec,
    own_hbm,
    other_hbm,
    line_hbm,
    mat_hbm,
    out_hbm,
    own_ref,
    other_ref,
    d_ref,
    rows_ref,
    mat_ref,
    out_ref,
    panel,
    d_rows,
    f_ref,
    g_ref,
    s_ref,
    u_ref,
    v_ref,
    sems,
    out_sems,
):
    k, p, q = scal[0], scal[1], scal[2]
    core = p % 2
    rows = 4 - r0
    tiles = rows + 2 - c0
    split = 4 * rows
    pairs = (
        (line_hbm.at[:, :, split : split + 6], d_ref),
        (own_hbm, own_ref),
        (other_hbm, other_ref),
        (line_hbm.at[:, :, 0:split], rows_ref),
        (mat_hbm, mat_ref),
    )
    fetches = [pltpu.make_async_copy(a, b, sems.at[n]) for n, (a, b) in enumerate(pairs)]
    for fetch in fetches:
        fetch.start()

    def store(r):
        at = pl.ds(pl.multiple_of(r * 1024, 1024), 1024)
        return pltpu.make_async_copy(out_ref.at[at], out_hbm.at[at], out_sems.at[r])

    def level_of(t, i):
        return lev[i % N_ROW, 4 * t + i // N_ROW]

    fetches[0].wait()
    for x in range(4):
        for z in range(8):
            d_rows[4 * z + x] = d_ref[x, z]

    def diag_tile(n):
        return jnp.concatenate([d_rows[:, 2 * n + h].reshape(B, HALF) for h in range(2)], axis=1)

    s_ref[...] = diag_tile(0)

    def factor(t, _):
        factor_tile(f_ref.at[t], s_ref, u_ref, v_ref)

        @pl.when(t == 0)
        def _():
            solved = by_level(dot_nt(diag_tile(1), f_ref[0, 1]), level_of(0, k + 1))
            g_ref[...] = solved
            s_ref[...] = diag_tile(2) - dot_nt(solved, solved)

        return 0

    lax.fori_loop(0, 2, factor, 0)

    for fetch in fetches[1:]:
        fetch.wait()
    for t in range(2):
        for h in range(2):
            lanes = slice(h * HALF, (h + 1) * HALF)
            for c in range(2 - c0):
                for part in range(2):
                    for y in range(8):
                        at = 8 * (16 * part + 2 * y)
                        for ref, side in ((own_ref, core), (other_ref, 1 - core)):
                            to = pl.ds(pl.multiple_of(at + 8 * side, 8), 8)
                            panel[t, rows + c, to, lanes] = ref[y, part, t, c, h]
            for r in range(rows):
                for x in range(4):
                    for z in range(8):
                        at = 8 * (4 * z + x)
                        panel[t, r, at : at + 8, lanes] = rows_ref[x, z, 2 * rows * t + 2 * r + h]

    def solve(n, _):
        i = jnp.where(n < rows, (n + r0) * N_ROW + p, (n - rows + c0) * N_COL + q)

        @pl.when(i > k)
        def _():
            panel[0, n] = by_level(dot_nt(panel[0, n], f_ref[0, 1]), level_of(0, i))
            level = level_of(1, i)

            @pl.when((i > k + 1) & (level == 2))
            def _():
                raw = panel[1, n] - dot_nt(panel[0, n], g_ref[...])
                panel[1, n] = dot_nt(raw, f_ref[1, 1])

            @pl.when((i > k + 1) & (level == 1))
            def _():
                raw = rounded(panel[1, n] - dot_narrow(panel[0, n], g_ref[...]))
                panel[1, n] = rounded(dot_nt(raw, f_ref[1, 1]))

        return 0

    lax.fori_loop(0, tiles, solve, 0)

    def trail(n, _):
        r, c = n // 2, n % 2
        i = r * N_ROW + p
        j = c * N_COL + q
        level = prec[r, c]
        active = (i >= j) & (j > k)
        row_at = jnp.maximum(r - r0, 0)
        col_at = rows + jnp.maximum(c - c0, 0)
        halves = [pl.ds(r * 1024 + c * 2 + h, B, stride=4) for h in range(2)]

        def put(value):
            for h in range(2):
                out_ref[halves[h], :] = value[:, h * HALF : (h + 1) * HALF]

        def get():
            return jnp.concatenate([mat_ref[halves[h], :] for h in range(2)], axis=1)

        own_first = (j == k) & (i > k)
        own_second = (j == k + 1) & (i > k + 1)
        diagonal = (i == j) & ((j == k) | (j == k + 1))
        plain = jnp.logical_not(own_first | own_second | diagonal)

        @pl.when(plain & (level == 2))
        def _():
            put(get())

            @pl.when(active)
            def _():
                put(get() - dot_nt(panel[0, row_at], panel[0, col_at]) - dot_nt(panel[1, row_at], panel[1, col_at]))

        @pl.when(plain & (level == 1))
        def _():
            put(rounded(get()))

            @pl.when(active)
            def _():
                once = rounded(rounded(get()) - dot_narrow(panel[0, row_at], panel[0, col_at]))
                put(rounded(once - dot_narrow(panel[1, row_at], panel[1, col_at])))

        @pl.when(plain & (level == 0))
        def _():
            put(jnp.zeros((B, B), f32))

        @pl.when(own_first)
        def _():
            put(panel[0, row_at])

        @pl.when(own_second)
        def _():
            put(panel[1, row_at])

        @pl.when(diagonal & (j == k))
        def _():
            put(f_ref[0, 0])

        @pl.when(diagonal & (j == k + 1))
        def _():
            put(f_ref[1, 0])

        @pl.when(c == 1)
        def _():
            store(r).start()

        return 0

    lax.fori_loop(0, 8, trail, 0)
    for r in range(4):
        store(r).wait()


def final(r0, c0, scal, lev, prec, own, other, line, mat):
    rows = 4 - r0
    return pl.pallas_call(
        functools.partial(final_kernel, r0, c0),
        in_specs=[SMEM, SMEM, SMEM] + [HBM] * 4,
        out_specs=HBM,
        out_shape=jax.ShapeDtypeStruct(mat.shape, f32),
        scratch_shapes=[
            pltpu.VMEM(own.shape, f32),
            pltpu.VMEM(other.shape, f32),
            pltpu.VMEM((4, 8, 6, 8, HALF), f32),
            pltpu.VMEM((4, 8, 4 * rows, 8, HALF), f32),
            pltpu.VMEM(mat.shape, f32),
            pltpu.VMEM(mat.shape, f32),
            pltpu.VMEM((2, rows + 2 - c0, B, B), f32),
            pltpu.VMEM((N_COL, 6, 8, HALF), f32),
            pltpu.VMEM((2, 2, B, B), f32),
            pltpu.VMEM((B, B), f32),
            pltpu.VMEM((B, B), f32),
            pltpu.VMEM((2, HALF, HALF), f32),
            pltpu.VMEM((2, HALF, HALF), f32),
            pltpu.SemaphoreType.DMA((5,)),
            pltpu.SemaphoreType.DMA((4,)),
        ],
        compiler_params=pltpu.CompilerParams(vmem_limit_bytes=24 << 20),
        cost_estimate=pl.CostEstimate(flops=4 * 10**10, bytes_accessed=10**7, transcendentals=0),
    )(scal, lev, prec, own, other, line, mat)


def cross_pairs(odd):
    pairs = []
    for p in range(N_ROW):
        for q in range(N_COL):
            low = q < N_ROW
            first = low != odd
            row = q if low else q - N_ROW
            col = p if first else p + N_ROW
            pairs.append((p * N_COL + q, row * N_COL + col))
    return pairs


def two_steps(r0, c0, scal, prec, mat):
    both = ("row", "col")
    z_groups = [[4 * z + x for z in range(8)] for x in range(4)]
    x_groups = [[4 * z + x for x in range(4)] for z in range(8)]
    y_groups = [[2 * y + c for y in range(8)] for c in range(2)]

    sent_diag, sent_bulk = pack(r0, scal, prec, mat)
    got_diag = lax.all_to_all(sent_diag, "col", 0, 0)
    seen = lax.all_gather(diag_parts(scal, got_diag), "row")
    got_bulk = lax.all_to_all(sent_bulk, "col", 0, 0)
    lev = seen[:, 4, :, 0].astype(jnp.int32)

    line, even, odd = route(r0, c0, scal, got_bulk, seen)
    line = lax.all_to_all(line, "col", 0, 0, axis_index_groups=z_groups)
    first = lax.ppermute(even, both, cross_pairs(False))
    second = lax.ppermute(odd, both, cross_pairs(True))
    line, first, second = lax.optimization_barrier((line, first, second))

    copies = jnp.broadcast_to(line[None], (4,) + line.shape)
    line = lax.all_to_all(copies, "col", 0, 0, axis_index_groups=x_groups)
    own = lax.all_gather(order_cols(scal, first, second), "row", axis_index_groups=y_groups)
    other = lax.ppermute(own, "row", [(i, i ^ 1) for i in range(N_ROW)])
    return final(r0, c0, scal, lev, prec, own, other, line, mat)


def per_device(matrix, precision, first_col):
    p = lax.axis_index("row")
    q = lax.axis_index("col")
    k = first_col[0]
    scal = jnp.stack([k, p, q]).astype(jnp.int32)
    prec = precision.reshape(4, 2)
    mat = matrix.reshape(4096, HALF)
    out = two_steps(0, 0, scal, prec, mat)
    return out.reshape(matrix.shape)


def solution(mesh):
    in_specs = (P(None, "row", None, None, "col", None), P(None, "row", None, "col"), P())
    out_specs = P(None, "row", None, None, "col", None)
    return jax.shard_map(
        per_device, mesh=mesh, in_specs=in_specs, out_specs=out_specs, check_vma=False
    )
```

```python
import functools

import jax
import jax.numpy as jnp
from jax import lax
from jax.experimental import pallas as pl
from jax.experimental.pallas import tpu as pltpu
from jax.sharding import PartitionSpec as P

HIGHEST = lax.Precision.HIGHEST
f32 = jnp.float32
N_ROW = 16
N_COL = 32
B = 256
HALF = 128
SMEM = pl.BlockSpec(memory_space=pltpu.SMEM)
VMEM = pl.BlockSpec(memory_space=pltpu.VMEM)
HBM = pl.BlockSpec(memory_space=pltpu.HBM)


def dot_nt(a, b):
    return lax.dot_general(
        a, b, (((1,), (1,)), ((), ())), precision=HIGHEST, preferred_element_type=f32
    )


def dot_nn(a, b):
    return lax.dot_general(
        a, b, (((1,), (0,)), ((), ())), precision=HIGHEST, preferred_element_type=f32
    )


def dot_narrow(a, b):
    return lax.dot_general(
        a.astype(jnp.bfloat16),
        b.astype(jnp.bfloat16),
        (((1,), (1,)), ((), ())),
        preferred_element_type=f32,
    )


def rounded(x):
    return x.astype(jnp.bfloat16).astype(f32)


def by_level(x, level):
    return jnp.where(level == 2, x, jnp.where(level == 1, rounded(x), 0.0))


def pack_kernel(r0, scal, prec, mat_ref, diag_ref, bulk_ref):
    k, p, q = scal[0], scal[1], scal[2]
    col = jnp.where(q == k % N_COL, k // N_COL, (k + 1) // N_COL)
    here_r = jnp.where(p == k % N_ROW, k // N_ROW, (k + 1) // N_ROW)
    sub = lax.broadcasted_iota(jnp.int32, (8, HALF), 0)
    levels = jnp.zeros((8, HALF), f32)
    for r in range(4):
        level = prec[r, col]
        levels = jnp.where(sub % 4 == r, level.astype(f32), levels)
    diag_ref[:, 2] = jnp.broadcast_to(levels[None], (32, 8, HALF))
    for r in range(r0, 4):
        for h in range(2):
            rows = mat_ref[pl.ds(r * 1024 + col * 2 + h, B, stride=4), :]
            rows = by_level(rows, prec[r, col]).reshape(32, 8, HALF)
            bulk_ref[:, (r - r0) * 2 + h] = rows

            @pl.when(here_r == r)
            def _():
                diag_ref[:, h] = rows


def pack(r0, scal, prec, mat):
    return pl.pallas_call(
        functools.partial(pack_kernel, r0),
        in_specs=[SMEM, SMEM, VMEM],
        out_specs=[VMEM, VMEM],
        out_shape=[
            jax.ShapeDtypeStruct((N_COL, 3, 8, HALF), f32),
            jax.ShapeDtypeStruct((N_COL, 8 - 2 * r0, 8, HALF), f32),
        ],
        compiler_params=pltpu.CompilerParams(vmem_limit_bytes=8 << 20),
    )(scal, prec, mat)


def diag_kernel(scal, first_ref, second_ref, out_ref):
    k, p = scal[0], scal[1]
    sub = lax.broadcasted_iota(jnp.int32, (8, HALF), 0)
    out_ref[0:2] = first_ref[0, 0:2]
    out_ref[2:4] = second_ref[0, 0:2]
    out_ref[4] = jnp.where(sub < 4, first_ref[0, 2], second_ref[0, 2])


def diag_parts(scal, received):
    block = (1, 3, 8, HALF)
    return pl.pallas_call(
        diag_kernel,
        grid_spec=pltpu.PrefetchScalarGridSpec(
            num_scalar_prefetch=1,
            grid=(1,),
            in_specs=[
                pl.BlockSpec(block, lambda _, s: (s[0] % N_COL, 0, 0, 0)),
                pl.BlockSpec(block, lambda _, s: ((s[0] + 1) % N_COL, 0, 0, 0)),
            ],
            out_specs=VMEM,
        ),
        out_shape=jax.ShapeDtypeStruct((5, 8, HALF), f32),
    )(scal, received, received)


def route_kernel(r0, c0, scal, first_ref, second_ref, here_ref, below_ref, line_ref, even_ref, odd_ref):
    low = scal[2] < N_ROW
    rows = 4 - r0
    for z in range(8):
        for t, ref in enumerate((first_ref, second_ref)):
            line_ref[z, 2 * rows * t : 2 * rows * (t + 1)] = ref[0]
        line_ref[z, 4 * rows : 4 * rows + 2] = here_ref[0, 0:2]
        line_ref[z, 4 * rows + 2 : 4 * rows + 6] = below_ref[0, 0:4]
    for t, ref in enumerate((first_ref, second_ref)):
        for c in range(c0, 2):
            for h in range(2):
                even = ref[0, 2 * max(2 * c - r0, 0) + h]
                odd = ref[0, 2 * (2 * c + 1 - r0) + h]
                even_ref[t, c - c0, h] = jnp.where(low, even, odd)
                odd_ref[t, c - c0, h] = jnp.where(low, odd, even)


def route(r0, c0, scal, received, seen):
    block = (1, 8 - 2 * r0, 8, HALF)
    part = (1, 5, 8, HALF)
    cross = jax.ShapeDtypeStruct((2, 2 - c0, 2, 8, HALF), f32)
    return pl.pallas_call(
        functools.partial(route_kernel, r0, c0),
        grid_spec=pltpu.PrefetchScalarGridSpec(
            num_scalar_prefetch=1,
            grid=(1,),
            in_specs=[
                pl.BlockSpec(block, lambda _, s: (s[0] % N_COL, 0, 0, 0)),
                pl.BlockSpec(block, lambda _, s: ((s[0] + 1) % N_COL, 0, 0, 0)),
                pl.BlockSpec(part, lambda _, s: (s[0] % N_ROW, 0, 0, 0)),
                pl.BlockSpec(part, lambda _, s: ((s[0] + 1) % N_ROW, 0, 0, 0)),
            ],
            out_specs=[VMEM, VMEM, VMEM],
        ),
        out_shape=[jax.ShapeDtypeStruct((8, 22 - 4 * r0, 8, HALF), f32), cross, cross],
    )(scal, received, received, seen, seen)


def cols_kernel(scal, first_ref, second_ref, out_ref):
    low = scal[2] < N_ROW
    first, second = first_ref[...], second_ref[...]
    out_ref[0] = jnp.where(low, first, second)
    out_ref[1] = jnp.where(low, second, first)


def order_cols(scal, first, second):
    return pl.pallas_call(
        cols_kernel,
        in_specs=[SMEM, VMEM, VMEM],
        out_specs=VMEM,
        out_shape=jax.ShapeDtypeStruct((2,) + first.shape, f32),
    )(scal, first, second)


def factor_half(block):
    groups, half = HALF // 8, HALF // 16
    sub = lax.broadcasted_iota(jnp.int32, (8, HALF), 0)
    lane = lax.broadcasted_iota(jnp.int32, (8, HALF), 1)
    up = [block[8 * g : 8 * g + 8, :] for g in range(groups)]
    inv = [jnp.where(lane == sub + 8 * g, 1.0, 0.0).astype(f32) for g in range(groups)]
    upper, lower_inv = [], []

    def row(x, j):
        return jnp.broadcast_to(x[j : j + 1, :], (8, HALF))

    def column(x, c):
        return jnp.broadcast_to(x[:, c : c + 1], (8, HALF))

    def pick(values):
        out = values[7]
        for i in range(6, -1, -1):
            out = jnp.where(sub == i, values[i], out)
        return out

    for start in (0, half):
        end = start + half
        ahead = None
        for b in range(start, end):
            here = ahead or [column(up[b], 8 * b + l) for l in range(8)]
            more = b + 1 < end
            if more:
                below = [column(up[b + 1], 8 * b + l) for l in range(8)]
                ahead = [column(up[b + 1], 8 * (b + 1) + l) for l in range(8)]
            pivots = [[row(here[l], i) for l in range(i + 1)] for i in range(8)]
            wide = [row(up[b], i) for i in range(8)]
            wide_inv = [row(inv[b], i) for i in range(8)]
            for j in range(8):
                recip = 1.0 / pivots[j][j]
                for i in range(j + 1, 8):
                    mult = pivots[i][j] * recip
                    for l in range(j + 1, i + 1):
                        pivots[i][l] = pivots[i][l] - mult * pivots[l][j]
                    wide[i] = wide[i] - mult * wide[j]
                    wide_inv[i] = wide_inv[i] - mult * wide_inv[j]
                if more:
                    mult = below[j] * recip
                    for l in range(8):
                        ahead[l] = ahead[l] - mult * row(below[j], l)
                    for l in range(j + 1, 8):
                        below[l] = below[l] - mult * pivots[l][j]
                    up[b + 1] = up[b + 1] - mult * wide[j]
                    inv[b + 1] = inv[b + 1] - mult * wide_inv[j]
            scale = lax.rsqrt(pick([pivots[i][i] for i in range(8)]))
            rows = pick(wide) * scale
            irows = pick(wide_inv) * scale
            upper.append(rows)
            lower_inv.append(irows)
            if b + 2 < end:
                row_each = [row(rows, j) for j in range(8)]
                irow_each = [row(irows, j) for j in range(8)]
                flipped = rows.T
                for g in range(b + 2, end):
                    part = flipped[8 * g : 8 * g + 8, :]
                    for j in range(8):
                        mult = column(part, j)
                        up[g] = up[g] - mult * row_each[j]
                        inv[g] = inv[g] - mult * irow_each[j]
        if end < groups:
            left = jnp.concatenate(upper, 0)
            both = jnp.concatenate([left, jnp.concatenate(lower_inv, 0)], 1)
            product = lax.dot_general(
                left[:, 8 * end :],
                both,
                (((0,), (0,)), ((), ())),
                precision=HIGHEST,
                preferred_element_type=f32,
            )
            for g in range(end, groups):
                at = 8 * (g - end)
                up[g] = up[g] - product[at : at + 8, :HALF]
                inv[g] = inv[g] - product[at : at + 8, HALF:]
    for b in range(groups):
        upper[b] = jnp.where(lane >= sub + 8 * b, upper[b], 0.0)
    return jnp.concatenate(upper, 0), jnp.concatenate(lower_inv, 0)


def factor_tile(out_ref, s_ref, u_ref, v_ref):
    def half(h, _):
        at = pl.ds(pl.multiple_of(h * HALF, HALF), HALF)
        u, v = factor_half(s_ref[at, at])
        u_ref[h] = u
        v_ref[h] = v

        @pl.when(h == 0)
        def _():
            l21 = dot_nt(s_ref[HALF:, 0:HALF], v)
            s_ref[HALF:, 0:HALF] = l21
            s_ref[HALF:, HALF:] = s_ref[HALF:, HALF:] - dot_nt(l21, l21)

        return 0

    lax.fori_loop(0, 2, half, 0)
    l21 = s_ref[HALF:, 0:HALF]
    zero = jnp.zeros((HALF, HALF), f32)
    v0, v1 = v_ref[0], v_ref[1]
    out_ref[0, 0:HALF, 0:HALF] = u_ref[0].T
    out_ref[0, 0:HALF, HALF:] = zero
    out_ref[0, HALF:, 0:HALF] = l21
    out_ref[0, HALF:, HALF:] = u_ref[1].T
    out_ref[1, 0:HALF, 0:HALF] = v0
    out_ref[1, 0:HALF, HALF:] = zero
    out_ref[1, HALF:, 0:HALF] = -dot_nn(v1, dot_nn(l21, v0))
    out_ref[1, HALF:, HALF:] = v1


def level_of(lev, t, i):
    return lev[i % N_ROW, 4 * t + i // N_ROW]


def factor_both(scal, lev, d_ref, d_rows, f_ref, g_ref, s_ref, u_ref, v_ref):
    for x in range(4):
        for z in range(8):
            d_rows[4 * z + x] = d_ref[x, z]

    def diag_tile(n):
        return jnp.concatenate([d_rows[:, 2 * n + h].reshape(B, HALF) for h in range(2)], axis=1)

    s_ref[...] = diag_tile(0)

    def factor(t, _):
        factor_tile(f_ref.at[t], s_ref, u_ref, v_ref)

        @pl.when(t == 0)
        def _():
            solved = by_level(dot_nt(diag_tile(1), f_ref[0, 1]), level_of(lev, 0, scal[0] + 1))
            g_ref[...] = solved
            s_ref[...] = diag_tile(2) - dot_nt(solved, solved)

        return 0

    lax.fori_loop(0, 2, factor, 0)


def place_rows(rows, rows_ref, panel):
    for t in range(2):
        for h in range(2):
            lanes = slice(h * HALF, (h + 1) * HALF)
            for r in range(rows):
                for x in range(4):
                    for z in range(8):
                        at = 8 * (4 * z + x)
                        panel[t, r, at : at + 8, lanes] = rows_ref[x, z, 2 * rows * t + 2 * r + h]


def solve_tiles(first, count, index_of, k, lev, panel, f_ref, g_ref):
    def solve(n, _):
        i = index_of(n)

        @pl.when(i > k)
        def _():
            panel[0, n] = by_level(dot_nt(panel[0, n], f_ref[0, 1]), level_of(lev, 0, i))
            level = level_of(lev, 1, i)

            @pl.when((i > k + 1) & (level == 2))
            def _():
                raw = panel[1, n] - dot_nt(panel[0, n], g_ref[...])
                panel[1, n] = dot_nt(raw, f_ref[1, 1])

            @pl.when((i > k + 1) & (level == 1))
            def _():
                raw = rounded(panel[1, n] - dot_narrow(panel[0, n], g_ref[...]))
                panel[1, n] = rounded(dot_nt(raw, f_ref[1, 1]))

        return 0

    lax.fori_loop(first, first + count, solve, 0)


def trail_tiles(r0, c0, scal, prec, panel, f_ref, mat_ref, out_ref, store):
    k, p, q = scal[0], scal[1], scal[2]

    def trail(n, _):
        r, c = n // 2, n % 2
        i = r * N_ROW + p
        j = c * N_COL + q
        level = prec[r, c]
        active = (i >= j) & (j > k)
        row_at = jnp.maximum(r - r0, 0)
        col_at = 4 - r0 + jnp.maximum(c - c0, 0)
        halves = [pl.ds(r * 1024 + c * 2 + h, B, stride=4) for h in range(2)]

        def put(value):
            for h in range(2):
                out_ref[halves[h], :] = value[:, h * HALF : (h + 1) * HALF]

        def get():
            return jnp.concatenate([mat_ref[halves[h], :] for h in range(2)], axis=1)

        own_first = (j == k) & (i > k)
        own_second = (j == k + 1) & (i > k + 1)
        diagonal = (i == j) & ((j == k) | (j == k + 1))
        plain = jnp.logical_not(own_first | own_second | diagonal)

        @pl.when(plain & (level == 2) & jnp.logical_not(active))
        def _():
            put(get())

        @pl.when(plain & (level == 2) & active)
        def _():
            first = dot_nt(panel[0, row_at], panel[0, col_at])
            put(get() - first - dot_nt(panel[1, row_at], panel[1, col_at]))

        @pl.when(plain & (level == 1) & jnp.logical_not(active))
        def _():
            put(rounded(get()))

        @pl.when(plain & (level == 1) & active)
        def _():
            once = rounded(rounded(get()) - dot_narrow(panel[0, row_at], panel[0, col_at]))
            put(rounded(once - dot_narrow(panel[1, row_at], panel[1, col_at])))

        @pl.when(plain & (level == 0))
        def _():
            put(jnp.zeros((B, B), f32))

        @pl.when(own_first)
        def _():
            put(panel[0, row_at])

        @pl.when(own_second)
        def _():
            put(panel[1, row_at])

        @pl.when(diagonal)
        def _():
            put(f_ref[j - k, 0])

        @pl.when(c == 1)
        def _():
            store(r).start()

        return 0

    lax.fori_loop(0, 8, trail, 0)
    for r in range(4):
        store(r).wait()


def store_to(out_ref, out_hbm, out_sems):
    def store(r):
        at = pl.ds(pl.multiple_of(r * 1024, 1024), 1024)
        return pltpu.make_async_copy(out_ref.at[at], out_hbm.at[at], out_sems.at[r])

    return store


def copies_in(pairs, sems):
    copies = [pltpu.make_async_copy(a, b, sems.at[n]) for n, (a, b) in enumerate(pairs)]
    for copy in copies:
        copy.start()
    return copies


FACTOR_SCRATCH = [
    pltpu.VMEM((N_COL, 6, 8, HALF), f32),
    pltpu.VMEM((2, 2, B, B), f32),
    pltpu.VMEM((B, B), f32),
    pltpu.VMEM((B, B), f32),
    pltpu.VMEM((2, HALF, HALF), f32),
    pltpu.VMEM((2, HALF, HALF), f32),
]


def final_kernel(r0, c0, n_cols, scal, lev, prec, *refs):
    col_hbm, (line_hbm, mat_hbm, out_hbm) = refs[:n_cols], refs[n_cols : n_cols + 3]
    refs = refs[n_cols + 3 :]
    col_refs, (d_ref, rows_ref, mat_ref, out_ref, panel) = refs[:n_cols], refs[n_cols : n_cols + 5]
    d_rows, f_ref, g_ref, s_ref, u_ref, v_ref, sems, out_sems = refs[n_cols + 5 :]
    k, p, q = scal[0], scal[1], scal[2]
    core = p % 2
    rows = 4 - r0
    split = 4 * rows
    pairs = [(line_hbm.at[:, :, split : split + 6], d_ref)]
    pairs += zip(col_hbm, col_refs)
    pairs += [(line_hbm.at[:, :, 0:split], rows_ref), (mat_hbm, mat_ref)]
    fetches = copies_in(pairs, sems)
    fetches[0].wait()
    factor_both(scal, lev, d_ref, d_rows, f_ref, g_ref, s_ref, u_ref, v_ref)
    for fetch in fetches[1:]:
        fetch.wait()
    place_rows(rows, rows_ref, panel)
    for t in range(2):
        for h in range(2):
            lanes = slice(h * HALF, (h + 1) * HALF)
            for c in range(2 - c0):
                for part in range(2):
                    if n_cols == 1:
                        at = slice(part * HALF, (part + 1) * HALF)
                        tile_half = col_refs[0][:, part, t, c, h].reshape(HALF, HALF)
                        panel[t, rows + c, at, lanes] = tile_half
                        continue
                    for y in range(8):
                        at = 8 * (16 * part + 2 * y)
                        for ref, side in zip(col_refs, (core, 1 - core)):
                            to = pl.ds(pl.multiple_of(at + 8 * side, 8), 8)
                            panel[t, rows + c, to, lanes] = ref[y, part, t, c, h]

    def index_of(n):
        return jnp.where(n < rows, (n + r0) * N_ROW + p, (n - rows + c0) * N_COL + q)

    solve_tiles(0, rows + 2 - c0, index_of, k, lev, panel, f_ref, g_ref)
    trail_tiles(
        r0, c0, scal, prec, panel, f_ref, mat_ref, out_ref, store_to(out_ref, out_hbm, out_sems)
    )


def final(r0, c0, scal, lev, prec, cols, line, mat):
    rows = 4 - r0
    return pl.pallas_call(
        functools.partial(final_kernel, r0, c0, len(cols)),
        in_specs=[SMEM, SMEM, SMEM] + [HBM] * (len(cols) + 2),
        out_specs=HBM,
        out_shape=jax.ShapeDtypeStruct(mat.shape, f32),
        scratch_shapes=[
            *[pltpu.VMEM(x.shape, f32) for x in cols],
            pltpu.VMEM((4, 8, 6, 8, HALF), f32),
            pltpu.VMEM((4, 8, 4 * rows, 8, HALF), f32),
            pltpu.VMEM(mat.shape, f32),
            pltpu.VMEM(mat.shape, f32),
            pltpu.VMEM((2, rows + 2 - c0, B, B), f32),
            *FACTOR_SCRATCH,
            pltpu.SemaphoreType.DMA((5,)),
            pltpu.SemaphoreType.DMA((4,)),
        ],
        compiler_params=pltpu.CompilerParams(vmem_limit_bytes=24 << 20),
        cost_estimate=pl.CostEstimate(flops=4 * 10**10, bytes_accessed=10**7, transcendentals=0),
    )(scal, lev, prec, *cols, line, mat)


def cross_pairs(odd):
    pairs = []
    for p in range(N_ROW):
        for q in range(N_COL):
            low = q < N_ROW
            first = low != odd
            row = q if low else q - N_ROW
            col = p if first else p + N_ROW
            pairs.append((p * N_COL + q, row * N_COL + col))
    return pairs


def two_steps(r0, c0, scal, prec, mat):
    both = ("row", "col")
    z_groups = [[4 * z + x for z in range(8)] for x in range(4)]
    x_groups = [[4 * z + x for x in range(4)] for z in range(8)]
    y_groups = [[2 * y + c for y in range(8)] for c in range(2)]

    sent_diag, sent_bulk = pack(r0, scal, prec, mat)
    got_diag = lax.all_to_all(sent_diag, "col", 0, 0)
    seen = lax.all_gather(diag_parts(scal, got_diag), "row")
    got_bulk = lax.all_to_all(sent_bulk, "col", 0, 0)
    lev = seen[:, 4, :, 0].astype(jnp.int32)

    line, even, odd = route(r0, c0, scal, got_bulk, seen)
    line = lax.all_to_all(line, "col", 0, 0, axis_index_groups=z_groups)
    first = lax.ppermute(even, both, cross_pairs(False))
    second = lax.ppermute(odd, both, cross_pairs(True))
    line, first, second = lax.optimization_barrier((line, first, second))

    copies = jnp.broadcast_to(line[None], (4,) + line.shape)
    line = lax.all_to_all(copies, "col", 0, 0, axis_index_groups=x_groups)
    parts = order_cols(scal, first, second)
    if c0 == 0:
        own = lax.all_gather(parts, "row", axis_index_groups=y_groups)
        other = lax.ppermute(own, "row", [(i, i ^ 1) for i in range(N_ROW)])
        cols = (own, other)
    else:
        cols = (lax.all_gather(parts, "row"),)
    return final(r0, c0, scal, lev, prec, cols, line, mat)


def per_device(matrix, precision, first_col):
    p = lax.axis_index("row")
    q = lax.axis_index("col")
    k = first_col[0]
    scal = jnp.stack([k, p, q]).astype(jnp.int32)
    prec = precision.reshape(4, 2)
    mat = matrix.reshape(4096, HALF)
    bands = [functools.partial(two_steps, r0, r0 // 2) for r0 in range(3)]
    out = lax.switch(k // N_ROW, bands, scal, prec, mat)
    return out.reshape(matrix.shape)


def solution(mesh):
    in_specs = (P(None, "row", None, None, "col", None), P(None, "row", None, "col"), P())
    out_specs = P(None, "row", None, None, "col", None)
    return jax.shard_map(
        per_device, mesh=mesh, in_specs=in_specs, out_specs=out_specs, check_vma=False
    )
```

```python
import functools

import jax
import jax.numpy as jnp
from jax import lax
from jax.experimental import pallas as pl
from jax.experimental.pallas import tpu as pltpu
from jax.sharding import PartitionSpec as P

HIGHEST = lax.Precision.HIGHEST
f32 = jnp.float32
N_ROW = 16
N_COL = 32
B = 256
HALF = 128
SMEM = pl.BlockSpec(memory_space=pltpu.SMEM)
VMEM = pl.BlockSpec(memory_space=pltpu.VMEM)
HBM = pl.BlockSpec(memory_space=pltpu.HBM)


def dot_nt(a, b):
    return lax.dot_general(
        a, b, (((1,), (1,)), ((), ())), precision=HIGHEST, preferred_element_type=f32
    )


def dot_nn(a, b):
    return lax.dot_general(
        a, b, (((1,), (0,)), ((), ())), precision=HIGHEST, preferred_element_type=f32
    )


def dot_narrow(a, b):
    return lax.dot_general(
        a.astype(jnp.bfloat16),
        b.astype(jnp.bfloat16),
        (((1,), (1,)), ((), ())),
        preferred_element_type=f32,
    )


def rounded(x):
    return x.astype(jnp.bfloat16).astype(f32)


def by_level(x, level):
    return jnp.where(level == 2, x, jnp.where(level == 1, rounded(x), 0.0))


def pack_diag_kernel(scal, prec, mat_hbm, diag_ref, rows_ref, sem):
    k, p, q = scal[0], scal[1], scal[2]
    col = jnp.where(q == k % N_COL, k // N_COL, (k + 1) // N_COL)
    here_r = jnp.where(p == k % N_ROW, k // N_ROW, (k + 1) // N_ROW)
    at = pl.ds(pl.multiple_of(here_r * 1024, 1024), 1024)
    fetch = pltpu.make_async_copy(mat_hbm.at[at], rows_ref, sem)
    fetch.start()
    sub = lax.broadcasted_iota(jnp.int32, (8, HALF), 0)
    levels = jnp.zeros((8, HALF), f32)
    for r in range(4):
        levels = jnp.where(sub % 4 == r, prec[col, r].astype(f32), levels)
    diag_ref[:, 2] = jnp.broadcast_to(levels[None], (32, 8, HALF))
    fetch.wait()
    for h in range(2):
        rows = rows_ref[pl.ds(col * 2 + h, B, stride=4), :]
        diag_ref[:, h] = by_level(rows, prec[col, here_r]).reshape(32, 8, HALF)


def pack_diag(scal, prec, mat):
    return pl.pallas_call(
        pack_diag_kernel,
        in_specs=[SMEM, SMEM, HBM],
        out_specs=VMEM,
        out_shape=jax.ShapeDtypeStruct((N_COL, 3, 8, HALF), f32),
        scratch_shapes=[pltpu.VMEM((1024, HALF), f32), pltpu.SemaphoreType.DMA(())],
        compiler_params=pltpu.CompilerParams(vmem_limit_bytes=8 << 20),
    )(scal, prec, mat)


def pack_bulk_kernel(r0, scal, prec, mat_ref, bulk_ref):
    k, q = scal[0], scal[2]
    col = jnp.where(q == k % N_COL, k // N_COL, (k + 1) // N_COL)
    for r in range(r0, 4):
        for h in range(2):
            rows = mat_ref[pl.ds(r * 1024 + col * 2 + h, B, stride=4), :]
            bulk_ref[:, (r - r0) * 2 + h] = by_level(rows, prec[col, r]).reshape(32, 8, HALF)


def pack_bulk(r0, scal, prec, mat):
    return pl.pallas_call(
        functools.partial(pack_bulk_kernel, r0),
        in_specs=[SMEM, SMEM, VMEM],
        out_specs=VMEM,
        out_shape=jax.ShapeDtypeStruct((N_COL, 8 - 2 * r0, 8, HALF), f32),
        compiler_params=pltpu.CompilerParams(vmem_limit_bytes=8 << 20),
        cost_estimate=pl.CostEstimate(flops=0, bytes_accessed=10**7, transcendentals=0),
    )(scal, prec, mat)


def diag_kernel(scal, got_ref, out_ref):
    k = scal[0]
    first, second = k % N_COL, (k + 1) % N_COL
    sub = lax.broadcasted_iota(jnp.int32, (8, HALF), 0)
    out_ref[0:2] = got_ref[first, 0:2]
    out_ref[2:4] = got_ref[second, 0:2]
    out_ref[4] = jnp.where(sub < 4, got_ref[first, 2], got_ref[second, 2])


def diag_parts(scal, received):
    return pl.pallas_call(
        diag_kernel,
        in_specs=[SMEM, VMEM],
        out_specs=VMEM,
        out_shape=jax.ShapeDtypeStruct((5, 8, HALF), f32),
    )(scal, received)


def route_kernel(r0, c0, scal, got_ref, seen_ref, line_ref, even_ref, odd_ref):
    k = scal[0]
    low = scal[2] < N_ROW
    rows = 4 - r0
    sources = (k % N_COL, (k + 1) % N_COL)
    for t, source in enumerate(sources):
        for c in range(c0, 2):
            for h in range(2):
                even = got_ref[source, 2 * max(2 * c - r0, 0) + h]
                odd = got_ref[source, 2 * (2 * c + 1 - r0) + h]
                even_ref[t, c - c0, h] = jnp.where(low, even, odd)
                odd_ref[t, c - c0, h] = jnp.where(low, odd, even)
    here = seen_ref[k % N_ROW, 0:2]
    below = seen_ref[(k + 1) % N_ROW, 0:4]
    for z in range(8):
        for t, source in enumerate(sources):
            line_ref[z, 2 * rows * t : 2 * rows * (t + 1)] = got_ref[source]
        line_ref[z, 4 * rows : 4 * rows + 2] = here
        line_ref[z, 4 * rows + 2 : 4 * rows + 6] = below


def route(r0, c0, scal, received, seen):
    cross = jax.ShapeDtypeStruct((2, 2 - c0, 2, 8, HALF), f32)
    line = jax.ShapeDtypeStruct((8, 22 - 4 * r0, 8, HALF), f32)
    return pl.pallas_call(
        functools.partial(route_kernel, r0, c0),
        in_specs=[SMEM, VMEM, VMEM],
        out_specs=[VMEM, VMEM, VMEM],
        out_shape=[line, cross, cross],
        compiler_params=pltpu.CompilerParams(vmem_limit_bytes=8 << 20),
    )(scal, received, seen)


def copies_kernel(line_ref, out_ref):
    for x in range(4):
        out_ref[x] = line_ref[...]


def line_copies(line):
    return pl.pallas_call(
        copies_kernel,
        in_specs=[VMEM],
        out_specs=VMEM,
        out_shape=jax.ShapeDtypeStruct((4,) + line.shape, f32),
        compiler_params=pltpu.CompilerParams(vmem_limit_bytes=8 << 20),
    )(line)


def cols_kernel(scal, first_ref, second_ref, out_ref):
    low = scal[2] < N_ROW
    first, second = first_ref[...], second_ref[...]
    out_ref[0] = jnp.where(low, first, second)
    out_ref[1] = jnp.where(low, second, first)


def order_cols(scal, first, second):
    return pl.pallas_call(
        cols_kernel,
        in_specs=[SMEM, VMEM, VMEM],
        out_specs=VMEM,
        out_shape=jax.ShapeDtypeStruct((2,) + first.shape, f32),
    )(scal, first, second)


def factor_half(block):
    groups, half = HALF // 8, HALF // 16
    sub = lax.broadcasted_iota(jnp.int32, (8, HALF), 0)
    lane = lax.broadcasted_iota(jnp.int32, (8, HALF), 1)
    up = [block[8 * g : 8 * g + 8, :] for g in range(groups)]
    inv = [jnp.where(lane == sub + 8 * g, 1.0, 0.0).astype(f32) for g in range(groups)]
    upper, lower_inv = [], []

    def row(x, j):
        return jnp.broadcast_to(x[j : j + 1, :], (8, HALF))

    def column(x, c):
        return jnp.broadcast_to(x[:, c : c + 1], (8, HALF))

    def pick(values):
        out = values[7]
        for i in range(6, -1, -1):
            out = jnp.where(sub == i, values[i], out)
        return out

    for start in (0, half):
        end = start + half
        ahead = None
        for b in range(start, end):
            here = ahead or [column(up[b], 8 * b + l) for l in range(8)]
            more = b + 1 < end
            if more:
                below = [column(up[b + 1], 8 * b + l) for l in range(8)]
                ahead = [column(up[b + 1], 8 * (b + 1) + l) for l in range(8)]
            pivots = [[row(here[l], i) for l in range(i + 1)] for i in range(8)]
            wide = [row(up[b], i) for i in range(8)]
            wide_inv = [row(inv[b], i) for i in range(8)]
            for j in range(8):
                recip = 1.0 / pivots[j][j]
                for i in range(j + 1, 8):
                    mult = pivots[i][j] * recip
                    for l in range(j + 1, i + 1):
                        pivots[i][l] = pivots[i][l] - mult * pivots[l][j]
                    wide[i] = wide[i] - mult * wide[j]
                    wide_inv[i] = wide_inv[i] - mult * wide_inv[j]
                if more:
                    mult = below[j] * recip
                    for l in range(8):
                        ahead[l] = ahead[l] - mult * row(below[j], l)
                    for l in range(j + 1, 8):
                        below[l] = below[l] - mult * pivots[l][j]
                    up[b + 1] = up[b + 1] - mult * wide[j]
                    inv[b + 1] = inv[b + 1] - mult * wide_inv[j]
            scale = lax.rsqrt(pick([pivots[i][i] for i in range(8)]))
            rows = pick(wide) * scale
            irows = pick(wide_inv) * scale
            upper.append(rows)
            lower_inv.append(irows)
            if b + 2 < end:
                row_each = [row(rows, j) for j in range(8)]
                irow_each = [row(irows, j) for j in range(8)]
                flipped = rows.T
                for g in range(b + 2, end):
                    part = flipped[8 * g : 8 * g + 8, :]
                    for j in range(8):
                        mult = column(part, j)
                        up[g] = up[g] - mult * row_each[j]
                        inv[g] = inv[g] - mult * irow_each[j]
        if end < groups:
            left = jnp.concatenate(upper, 0)
            both = jnp.concatenate([left, jnp.concatenate(lower_inv, 0)], 1)
            product = lax.dot_general(
                left[:, 8 * end :],
                both,
                (((0,), (0,)), ((), ())),
                precision=HIGHEST,
                preferred_element_type=f32,
            )
            for g in range(end, groups):
                at = 8 * (g - end)
                up[g] = up[g] - product[at : at + 8, :HALF]
                inv[g] = inv[g] - product[at : at + 8, HALF:]
    for b in range(groups):
        upper[b] = jnp.where(lane >= sub + 8 * b, upper[b], 0.0)
    return jnp.concatenate(upper, 0), jnp.concatenate(lower_inv, 0)


def factor_tile(out_ref, s_ref, u_ref, v_ref):
    def half(h, _):
        at = pl.ds(pl.multiple_of(h * HALF, HALF), HALF)
        u, v = factor_half(s_ref[at, at])
        u_ref[h] = u
        v_ref[h] = v

        @pl.when(h == 0)
        def _():
            l21 = dot_nt(s_ref[HALF:, 0:HALF], v)
            s_ref[HALF:, 0:HALF] = l21
            s_ref[HALF:, HALF:] = s_ref[HALF:, HALF:] - dot_nt(l21, l21)

        return 0

    lax.fori_loop(0, 2, half, 0)
    l21 = s_ref[HALF:, 0:HALF]
    zero = jnp.zeros((HALF, HALF), f32)
    v0, v1 = v_ref[0], v_ref[1]
    out_ref[0, 0:HALF, 0:HALF] = u_ref[0].T
    out_ref[0, 0:HALF, HALF:] = zero
    out_ref[0, HALF:, 0:HALF] = l21
    out_ref[0, HALF:, HALF:] = u_ref[1].T
    out_ref[1, 0:HALF, 0:HALF] = v0
    out_ref[1, 0:HALF, HALF:] = zero
    out_ref[1, HALF:, 0:HALF] = -dot_nn(v1, dot_nn(l21, v0))
    out_ref[1, HALF:, HALF:] = v1


def level_of(lev, t, i):
    return lev[i % N_ROW, 4 * t + i // N_ROW]


def factor_both(scal, lev, d_ref, d_rows, f_ref, g_ref, s_ref, u_ref, v_ref):
    for x in range(4):
        for z in range(8):
            d_rows[4 * z + x] = d_ref[x, z]

    def diag_tile(n):
        return jnp.concatenate([d_rows[:, 2 * n + h].reshape(B, HALF) for h in range(2)], axis=1)

    s_ref[...] = diag_tile(0)

    def factor(t, _):
        factor_tile(f_ref.at[t], s_ref, u_ref, v_ref)

        @pl.when(t == 0)
        def _():
            solved = by_level(dot_nt(diag_tile(1), f_ref[0, 1]), level_of(lev, 0, scal[0] + 1))
            g_ref[...] = solved
            s_ref[...] = diag_tile(2) - dot_nt(solved, solved)

        return 0

    lax.fori_loop(0, 2, factor, 0)


def place_rows(rows, rows_ref, panel):
    for t in range(2):
        for h in range(2):
            lanes = slice(h * HALF, (h + 1) * HALF)
            for r in range(rows):
                for x in range(4):
                    for z in range(8):
                        at = 8 * (4 * z + x)
                        panel[t, r, at : at + 8, lanes] = rows_ref[x, z, 2 * rows * t + 2 * r + h]


def solve_tiles(first, count, index_of, k, lev, panel, f_ref, g_ref):
    def solve(n, _):
        i = index_of(n)

        @pl.when(i > k)
        def _():
            panel[0, n] = by_level(dot_nt(panel[0, n], f_ref[0, 1]), level_of(lev, 0, i))
            level = level_of(lev, 1, i)

            @pl.when((i > k + 1) & (level == 2))
            def _():
                raw = panel[1, n] - dot_nt(panel[0, n], g_ref[...])
                panel[1, n] = dot_nt(raw, f_ref[1, 1])

            @pl.when((i > k + 1) & (level == 1))
            def _():
                raw = rounded(panel[1, n] - dot_narrow(panel[0, n], g_ref[...]))
                panel[1, n] = rounded(dot_nt(raw, f_ref[1, 1]))

        return 0

    lax.fori_loop(first, first + count, solve, 0)


def trail_tiles(r0, c0, scal, prec, panel, f_ref, mat_ref, out_ref, store):
    k, p, q = scal[0], scal[1], scal[2]

    def trail(n, _):
        r, c = n // 2, n % 2
        i = r * N_ROW + p
        j = c * N_COL + q
        level = prec[c, r]
        active = (i >= j) & (j > k)
        row_at = jnp.maximum(r - r0, 0)
        col_at = 4 - r0 + jnp.maximum(c - c0, 0)
        halves = [pl.ds(r * 1024 + c * 2 + h, B, stride=4) for h in range(2)]

        def put(value):
            for h in range(2):
                out_ref[halves[h], :] = value[:, h * HALF : (h + 1) * HALF]

        def get():
            return jnp.concatenate([mat_ref[halves[h], :] for h in range(2)], axis=1)

        own_first = (j == k) & (i > k)
        own_second = (j == k + 1) & (i > k + 1)
        diagonal = (i == j) & ((j == k) | (j == k + 1))
        plain = jnp.logical_not(own_first | own_second | diagonal)

        @pl.when(plain & (level == 2) & jnp.logical_not(active))
        def _():
            put(get())

        @pl.when(plain & (level == 2) & active)
        def _():
            first = dot_nt(panel[0, row_at], panel[0, col_at])
            put(get() - first - dot_nt(panel[1, row_at], panel[1, col_at]))

        @pl.when(plain & (level == 1) & jnp.logical_not(active))
        def _():
            put(rounded(get()))

        @pl.when(plain & (level == 1) & active)
        def _():
            once = rounded(rounded(get()) - dot_narrow(panel[0, row_at], panel[0, col_at]))
            put(rounded(once - dot_narrow(panel[1, row_at], panel[1, col_at])))

        @pl.when(plain & (level == 0))
        def _():
            put(jnp.zeros((B, B), f32))

        @pl.when(own_first)
        def _():
            put(panel[0, row_at])

        @pl.when(own_second)
        def _():
            put(panel[1, row_at])

        @pl.when(diagonal)
        def _():
            put(f_ref[j - k, 0])

        @pl.when(c == 1)
        def _():
            store(r).start()

        return 0

    lax.fori_loop(0, 8, trail, 0)
    for r in range(4):
        store(r).wait()


def store_to(out_ref, out_hbm, out_sems):
    def store(r):
        at = pl.ds(pl.multiple_of(r * 1024, 1024), 1024)
        return pltpu.make_async_copy(out_ref.at[at], out_hbm.at[at], out_sems.at[r])

    return store


def copies_in(pairs, sems):
    copies = [pltpu.make_async_copy(a, b, sems.at[n]) for n, (a, b) in enumerate(pairs)]
    for copy in copies:
        copy.start()
    return copies


FACTOR_SCRATCH = [
    pltpu.VMEM((N_COL, 6, 8, HALF), f32),
    pltpu.VMEM((2, 2, B, B), f32),
    pltpu.VMEM((B, B), f32),
    pltpu.VMEM((B, B), f32),
    pltpu.VMEM((2, HALF, HALF), f32),
    pltpu.VMEM((2, HALF, HALF), f32),
]


def final_kernel(r0, c0, n_cols, scal, lev, prec, *refs):
    col_hbm, (line_hbm, mat_hbm, out_hbm) = refs[:n_cols], refs[n_cols : n_cols + 3]
    refs = refs[n_cols + 3 :]
    col_refs, (d_ref, rows_ref, mat_ref, out_ref, panel) = refs[:n_cols], refs[n_cols : n_cols + 5]
    d_rows, f_ref, g_ref, s_ref, u_ref, v_ref, sems, out_sems = refs[n_cols + 5 :]
    k, p, q = scal[0], scal[1], scal[2]
    core = p % 2
    rows = 4 - r0
    split = 4 * rows
    pairs = [(line_hbm.at[:, :, split : split + 6], d_ref)]
    pairs += zip(col_hbm, col_refs)
    pairs += [(line_hbm.at[:, :, 0:split], rows_ref), (mat_hbm, mat_ref)]
    fetches = copies_in(pairs, sems)
    fetches[0].wait()
    factor_both(scal, lev, d_ref, d_rows, f_ref, g_ref, s_ref, u_ref, v_ref)
    for fetch in fetches[1:]:
        fetch.wait()
    place_rows(rows, rows_ref, panel)
    for t in range(2):
        for h in range(2):
            lanes = slice(h * HALF, (h + 1) * HALF)
            for c in range(2 - c0):
                for part in range(2):
                    if n_cols == 1:
                        at = slice(part * HALF, (part + 1) * HALF)
                        tile_half = col_refs[0][:, part, t, c, h].reshape(HALF, HALF)
                        panel[t, rows + c, at, lanes] = tile_half
                        continue
                    for y in range(8):
                        at = 8 * (16 * part + 2 * y)
                        for ref, side in zip(col_refs, (core, 1 - core)):
                            to = pl.ds(pl.multiple_of(at + 8 * side, 8), 8)
                            panel[t, rows + c, to, lanes] = ref[y, part, t, c, h]

    def index_of(n):
        return jnp.where(n < rows, (n + r0) * N_ROW + p, (n - rows + c0) * N_COL + q)

    solve_tiles(0, rows + 2 - c0, index_of, k, lev, panel, f_ref, g_ref)
    trail_tiles(
        r0, c0, scal, prec, panel, f_ref, mat_ref, out_ref, store_to(out_ref, out_hbm, out_sems)
    )


def final(r0, c0, scal, lev, prec, cols, line, mat):
    rows = 4 - r0
    return pl.pallas_call(
        functools.partial(final_kernel, r0, c0, len(cols)),
        in_specs=[SMEM, SMEM, SMEM] + [HBM] * (len(cols) + 2),
        out_specs=HBM,
        out_shape=pltpu.HBM(mat.shape, f32),
        scratch_shapes=[
            *[pltpu.VMEM(x.shape, f32) for x in cols],
            pltpu.VMEM((4, 8, 6, 8, HALF), f32),
            pltpu.VMEM((4, 8, 4 * rows, 8, HALF), f32),
            pltpu.VMEM(mat.shape, f32),
            pltpu.VMEM(mat.shape, f32),
            pltpu.VMEM((2, rows + 2 - c0, B, B), f32),
            *FACTOR_SCRATCH,
            pltpu.SemaphoreType.DMA((5,)),
            pltpu.SemaphoreType.DMA((4,)),
        ],
        compiler_params=pltpu.CompilerParams(vmem_limit_bytes=24 << 20),
        cost_estimate=pl.CostEstimate(flops=4 * 10**10, bytes_accessed=10**7, transcendentals=0),
    )(scal, lev, prec, *cols, line, mat)


def cross_pairs(odd):
    pairs = []
    for p in range(N_ROW):
        for q in range(N_COL):
            low = q < N_ROW
            first = low != odd
            row = q if low else q - N_ROW
            col = p if first else p + N_ROW
            pairs.append((p * N_COL + q, row * N_COL + col))
    return pairs


def two_steps(r0, c0, scal, prec, mat):
    both = ("row", "col")
    z_groups = [[4 * z + x for z in range(8)] for x in range(4)]
    x_groups = [[4 * z + x for x in range(4)] for z in range(8)]
    y_groups = [[2 * y + c for y in range(8)] for c in range(2)]

    got_diag = lax.all_to_all(pack_diag(scal, prec, mat), "col", 0, 0)
    seen = lax.all_gather(diag_parts(scal, got_diag), "row")
    got_bulk = lax.all_to_all(pack_bulk(r0, scal, prec, mat), "col", 0, 0)
    lev = seen[:, 4, :, 0].astype(jnp.int32)

    line, even, odd = route(r0, c0, scal, got_bulk, seen)
    line = lax.all_to_all(line, "col", 0, 0, axis_index_groups=z_groups)
    first = lax.ppermute(even, both, cross_pairs(False))
    second = lax.ppermute(odd, both, cross_pairs(True))
    line, first, second, lev = lax.optimization_barrier((line, first, second, lev))

    line = lax.all_to_all(line_copies(line), "col", 0, 0, axis_index_groups=x_groups)
    parts = order_cols(scal, first, second)
    if c0 == 0:
        own = lax.all_gather(parts, "row", axis_index_groups=y_groups)
        other = lax.ppermute(own, "row", [(i, i ^ 1) for i in range(N_ROW)])
        cols = (own, other)
    else:
        cols = (lax.all_gather(parts, "row"),)
    return final(r0, c0, scal, lev, prec, cols, line, mat)


def per_device(matrix, precision, first_col):
    p = lax.axis_index("row")
    q = lax.axis_index("col")
    k = first_col[0]
    scal = jnp.stack([k, p, q]).astype(jnp.int32)
    prec = precision.reshape(4, 2).T
    mat = matrix.reshape(4096, HALF)
    bands = [functools.partial(two_steps, r0, r0 // 2) for r0 in range(3)]
    out = lax.switch(k // N_ROW, bands, scal, prec, mat)
    return out.reshape(matrix.shape)


def solution(mesh):
    in_specs = (P(None, "row", None, None, "col", None), P(None, "row", None, "col"), P())
    out_specs = P(None, "row", None, None, "col", None)
    return jax.shard_map(
        per_device, mesh=mesh, in_specs=in_specs, out_specs=out_specs, check_vma=False
    )
```

```python
import functools

import jax
import jax.numpy as jnp
from jax import lax
from jax.experimental import pallas as pl
from jax.experimental.pallas import tpu as pltpu
from jax.sharding import PartitionSpec as P

HIGHEST = lax.Precision.HIGHEST
f32 = jnp.float32
N_ROW = 16
N_COL = 32
B = 256
HALF = 128
SMEM = pl.BlockSpec(memory_space=pltpu.SMEM)
VMEM = pl.BlockSpec(memory_space=pltpu.VMEM)
HBM = pl.BlockSpec(memory_space=pltpu.HBM)


def dot_nt(a, b):
    return lax.dot_general(
        a, b, (((1,), (1,)), ((), ())), precision=HIGHEST, preferred_element_type=f32
    )


def dot_nn(a, b):
    return lax.dot_general(
        a, b, (((1,), (0,)), ((), ())), precision=HIGHEST, preferred_element_type=f32
    )


def dot_narrow(a, b):
    return lax.dot_general(
        a.astype(jnp.bfloat16),
        b.astype(jnp.bfloat16),
        (((1,), (1,)), ((), ())),
        preferred_element_type=f32,
    )


def rounded(x):
    return x.astype(jnp.bfloat16).astype(f32)


def by_level(x, level):
    return jnp.where(level == 2, x, jnp.where(level == 1, rounded(x), 0.0))


def pack_diag_kernel(scal, prec, mat_hbm, diag_ref, rows_ref, sem):
    k, p, q = scal[0], scal[1], scal[2]
    col = jnp.where(q == k % N_COL, k // N_COL, (k + 1) // N_COL)
    here_r = jnp.where(p == k % N_ROW, k // N_ROW, (k + 1) // N_ROW)
    at = pl.ds(pl.multiple_of(here_r * 1024, 1024), 1024)
    fetch = pltpu.make_async_copy(mat_hbm.at[at], rows_ref, sem)
    fetch.start()
    sub = lax.broadcasted_iota(jnp.int32, (8, HALF), 0)
    levels = jnp.zeros((8, HALF), f32)
    for r in range(4):
        levels = jnp.where(sub % 4 == r, prec[col, r].astype(f32), levels)
    diag_ref[:, 2] = jnp.broadcast_to(levels[None], (32, 8, HALF))
    fetch.wait()
    for h in range(2):
        rows = rows_ref[pl.ds(col * 2 + h, B, stride=4), :]
        diag_ref[:, h] = by_level(rows, prec[col, here_r]).reshape(32, 8, HALF)


def pack_diag(scal, prec, mat):
    return pl.pallas_call(
        pack_diag_kernel,
        in_specs=[SMEM, SMEM, HBM],
        out_specs=VMEM,
        out_shape=jax.ShapeDtypeStruct((N_COL, 3, 8, HALF), f32),
        scratch_shapes=[pltpu.VMEM((1024, HALF), f32), pltpu.SemaphoreType.DMA(())],
        compiler_params=pltpu.CompilerParams(vmem_limit_bytes=8 << 20),
    )(scal, prec, mat)


def pack_bulk_kernel(r0, scal, prec, mat_ref, bulk_ref):
    k, q = scal[0], scal[2]
    col = jnp.where(q == k % N_COL, k // N_COL, (k + 1) // N_COL)
    for r in range(r0, 4):
        for h in range(2):
            rows = mat_ref[pl.ds(r * 1024 + col * 2 + h, B, stride=4), :]
            bulk_ref[:, (r - r0) * 2 + h] = by_level(rows, prec[col, r]).reshape(32, 8, HALF)


def pack_bulk(r0, scal, prec, mat):
    return pl.pallas_call(
        functools.partial(pack_bulk_kernel, r0),
        in_specs=[SMEM, SMEM, VMEM],
        out_specs=VMEM,
        out_shape=jax.ShapeDtypeStruct((N_COL, 8 - 2 * r0, 8, HALF), f32),
        compiler_params=pltpu.CompilerParams(vmem_limit_bytes=8 << 20),
        cost_estimate=pl.CostEstimate(flops=0, bytes_accessed=10**7, transcendentals=0),
    )(scal, prec, mat)


def diag_kernel(scal, got_ref, out_ref):
    k = scal[0]
    first, second = k % N_COL, (k + 1) % N_COL
    sub = lax.broadcasted_iota(jnp.int32, (8, HALF), 0)
    out_ref[0:2] = got_ref[first, 0:2]
    out_ref[2:4] = got_ref[second, 0:2]
    out_ref[4] = jnp.where(sub < 4, got_ref[first, 2], got_ref[second, 2])


def diag_parts(scal, received):
    return pl.pallas_call(
        diag_kernel,
        in_specs=[SMEM, VMEM],
        out_specs=VMEM,
        out_shape=jax.ShapeDtypeStruct((5, 8, HALF), f32),
    )(scal, received)


def route_kernel(r0, c0, scal, got_ref, seen_ref, line_ref, even_ref, odd_ref):
    k = scal[0]
    low = scal[2] < N_ROW
    rows = 4 - r0
    sources = (k % N_COL, (k + 1) % N_COL)
    for t, source in enumerate(sources):
        for c in range(c0, 2):
            for h in range(2):
                even = got_ref[source, 2 * max(2 * c - r0, 0) + h]
                odd = got_ref[source, 2 * (2 * c + 1 - r0) + h]
                even_ref[t, c - c0, h] = jnp.where(low, even, odd)
                odd_ref[t, c - c0, h] = jnp.where(low, odd, even)
    here = seen_ref[k % N_ROW, 0:2]
    below = seen_ref[(k + 1) % N_ROW, 0:4]
    for z in range(8):
        for t, source in enumerate(sources):
            line_ref[z, 2 * rows * t : 2 * rows * (t + 1)] = got_ref[source]
        line_ref[z, 4 * rows : 4 * rows + 2] = here
        line_ref[z, 4 * rows + 2 : 4 * rows + 6] = below


def route(r0, c0, scal, received, seen):
    cross = jax.ShapeDtypeStruct((2, 2 - c0, 2, 8, HALF), f32)
    line = jax.ShapeDtypeStruct((8, 22 - 4 * r0, 8, HALF), f32)
    return pl.pallas_call(
        functools.partial(route_kernel, r0, c0),
        in_specs=[SMEM, VMEM, VMEM],
        out_specs=[VMEM, VMEM, VMEM],
        out_shape=[line, cross, cross],
        compiler_params=pltpu.CompilerParams(vmem_limit_bytes=8 << 20),
    )(scal, received, seen)


def copies_kernel(line_ref, out_ref):
    for x in range(4):
        out_ref[x] = line_ref[...]


def line_copies(line):
    return pl.pallas_call(
        copies_kernel,
        in_specs=[VMEM],
        out_specs=VMEM,
        out_shape=jax.ShapeDtypeStruct((4,) + line.shape, f32),
        compiler_params=pltpu.CompilerParams(vmem_limit_bytes=8 << 20),
    )(line)


def cols_kernel(scal, first_ref, second_ref, out_ref):
    low = scal[2] < N_ROW
    first, second = first_ref[...], second_ref[...]
    out_ref[0] = jnp.where(low, first, second)
    out_ref[1] = jnp.where(low, second, first)


def order_cols(scal, first, second):
    return pl.pallas_call(
        cols_kernel,
        in_specs=[SMEM, VMEM, VMEM],
        out_specs=VMEM,
        out_shape=jax.ShapeDtypeStruct((2,) + first.shape, f32),
    )(scal, first, second)


def factor_half(block):
    groups, half = HALF // 8, HALF // 16
    sub = lax.broadcasted_iota(jnp.int32, (8, HALF), 0)
    lane = lax.broadcasted_iota(jnp.int32, (8, HALF), 1)
    up = [block[8 * g : 8 * g + 8, :] for g in range(groups)]
    inv = [jnp.where(lane == sub + 8 * g, 1.0, 0.0).astype(f32) for g in range(groups)]
    upper, lower_inv = [], []

    def row(x, j):
        return jnp.broadcast_to(x[j : j + 1, :], (8, HALF))

    def column(x, c):
        return jnp.broadcast_to(x[:, c : c + 1], (8, HALF))

    def pick(values):
        out = values[7]
        for i in range(6, -1, -1):
            out = jnp.where(sub == i, values[i], out)
        return out

    for start in (0, half):
        end = start + half
        ahead = None
        for b in range(start, end):
            here = ahead or [column(up[b], 8 * b + l) for l in range(8)]
            more = b + 1 < end
            if more:
                below = [column(up[b + 1], 8 * b + l) for l in range(8)]
                ahead = [column(up[b + 1], 8 * (b + 1) + l) for l in range(8)]
            pivots = [[row(here[l], i) for l in range(i + 1)] for i in range(8)]
            wide = [row(up[b], i) for i in range(8)]
            wide_inv = [row(inv[b], i) for i in range(8)]
            for j in range(8):
                recip = 1.0 / pivots[j][j]
                for i in range(j + 1, 8):
                    mult = pivots[i][j] * recip
                    for l in range(j + 1, i + 1):
                        pivots[i][l] = pivots[i][l] - mult * pivots[l][j]
                    wide[i] = wide[i] - mult * wide[j]
                    wide_inv[i] = wide_inv[i] - mult * wide_inv[j]
                if more:
                    mult = below[j] * recip
                    for l in range(8):
                        ahead[l] = ahead[l] - mult * row(below[j], l)
                    for l in range(j + 1, 8):
                        below[l] = below[l] - mult * pivots[l][j]
                    up[b + 1] = up[b + 1] - mult * wide[j]
                    inv[b + 1] = inv[b + 1] - mult * wide_inv[j]
            scale = lax.rsqrt(pick([pivots[i][i] for i in range(8)]))
            rows = pick(wide) * scale
            irows = pick(wide_inv) * scale
            upper.append(rows)
            lower_inv.append(irows)
            if b + 2 < end:
                row_each = [row(rows, j) for j in range(8)]
                irow_each = [row(irows, j) for j in range(8)]
                flipped = rows.T
                for g in range(b + 2, end):
                    part = flipped[8 * g : 8 * g + 8, :]
                    for j in range(8):
                        mult = column(part, j)
                        up[g] = up[g] - mult * row_each[j]
                        inv[g] = inv[g] - mult * irow_each[j]
        if end < groups:
            left = jnp.concatenate(upper, 0)
            both = jnp.concatenate([left, jnp.concatenate(lower_inv, 0)], 1)
            product = lax.dot_general(
                left[:, 8 * end :],
                both,
                (((0,), (0,)), ((), ())),
                precision=HIGHEST,
                preferred_element_type=f32,
            )
            for g in range(end, groups):
                at = 8 * (g - end)
                up[g] = up[g] - product[at : at + 8, :HALF]
                inv[g] = inv[g] - product[at : at + 8, HALF:]
    for b in range(groups):
        upper[b] = jnp.where(lane >= sub + 8 * b, upper[b], 0.0)
    return jnp.concatenate(upper, 0), jnp.concatenate(lower_inv, 0)


def factor_tile(out_ref, s_ref, u_ref, v_ref):
    def half(h, _):
        at = pl.ds(pl.multiple_of(h * HALF, HALF), HALF)
        u, v = factor_half(s_ref[at, at])
        u_ref[h] = u
        v_ref[h] = v

        @pl.when(h == 0)
        def _():
            l21 = dot_nt(s_ref[HALF:, 0:HALF], v)
            s_ref[HALF:, 0:HALF] = l21
            s_ref[HALF:, HALF:] = s_ref[HALF:, HALF:] - dot_nt(l21, l21)

        return 0

    lax.fori_loop(0, 2, half, 0)
    l21 = s_ref[HALF:, 0:HALF]
    zero = jnp.zeros((HALF, HALF), f32)
    v0, v1 = v_ref[0], v_ref[1]
    out_ref[0, 0:HALF, 0:HALF] = u_ref[0].T
    out_ref[0, 0:HALF, HALF:] = zero
    out_ref[0, HALF:, 0:HALF] = l21
    out_ref[0, HALF:, HALF:] = u_ref[1].T
    out_ref[1, 0:HALF, 0:HALF] = v0
    out_ref[1, 0:HALF, HALF:] = zero
    out_ref[1, HALF:, 0:HALF] = -dot_nn(v1, dot_nn(l21, v0))
    out_ref[1, HALF:, HALF:] = v1


def level_of(lev, t, i):
    return lev[i % N_ROW, 4 * t + i // N_ROW]


def factor_first(scal, lev, d_ref, d_rows, f_ref, g_ref, s_ref, u_ref, v_ref):
    for x in range(4):
        for z in range(8):
            d_rows[4 * z + x] = d_ref[x, z]

    def diag_tile(n):
        return jnp.concatenate([d_rows[:, 2 * n + h].reshape(B, HALF) for h in range(2)], axis=1)

    s_ref[...] = diag_tile(0)
    factor_tile(f_ref.at[0], s_ref, u_ref, v_ref)
    solved = by_level(dot_nt(diag_tile(1), f_ref[0, 1]), level_of(lev, 0, scal[0] + 1))
    g_ref[...] = solved
    s_ref[...] = diag_tile(2) - dot_nt(solved, solved)


def first_panel(tiles, index_of, lev, panel, f_ref, g_ref):
    for n in range(tiles):
        i = index_of(n)
        solved = by_level(dot_nt(panel[0, n], f_ref[0, 1]), level_of(lev, 0, i))
        panel[0, n] = solved
        level = level_of(lev, 1, i)
        narrow = level == 1
        other = g_ref[...]
        left = jnp.where(narrow, rounded(solved), solved)
        right = jnp.where(narrow, rounded(other), other)
        panel[1, n] = by_level(panel[1, n] - dot_nt(left, right), level)


def factor_second(f_ref, s_ref):
    u0, v0 = factor_half(s_ref[0:HALF, 0:HALF])
    l21 = dot_nt(s_ref[HALF:, 0:HALF], v0)
    u1, v1 = factor_half(s_ref[HALF:, HALF:] - dot_nt(l21, l21))
    zero = jnp.zeros((HALF, HALF), f32)
    f_ref[1, 0, 0:HALF, 0:HALF] = u0.T
    f_ref[1, 0, 0:HALF, HALF:] = zero
    f_ref[1, 0, HALF:, 0:HALF] = l21
    f_ref[1, 0, HALF:, HALF:] = u1.T
    f_ref[1, 1, 0:HALF, 0:HALF] = v0
    f_ref[1, 1, 0:HALF, HALF:] = zero
    f_ref[1, 1, HALF:, 0:HALF] = -dot_nn(v1, dot_nn(l21, v0))
    f_ref[1, 1, HALF:, HALF:] = v1


def place_rows(rows, rows_ref, panel):
    for t in range(2):
        for h in range(2):
            lanes = slice(h * HALF, (h + 1) * HALF)
            for r in range(rows):
                for x in range(4):
                    for z in range(8):
                        at = 8 * (4 * z + x)
                        panel[t, r, at : at + 8, lanes] = rows_ref[x, z, 2 * rows * t + 2 * r + h]


def second_panel(tiles, index_of, k, lev, panel, f_ref):
    def solve(n, _):
        i = index_of(n)

        @pl.when(i > k + 1)
        def _():
            panel[1, n] = by_level(dot_nt(panel[1, n], f_ref[1, 1]), level_of(lev, 1, i))

        return 0

    lax.fori_loop(0, tiles, solve, 0)


def trail_tiles(r0, c0, scal, prec, panel, f_ref, mat_ref, out_ref, store):
    k, p, q = scal[0], scal[1], scal[2]

    def trail(n, _):
        r, c = n // 2, n % 2
        i = r * N_ROW + p
        j = c * N_COL + q
        level = prec[c, r]
        active = (i >= j) & (j > k)
        row_at = jnp.maximum(r - r0, 0)
        col_at = 4 - r0 + jnp.maximum(c - c0, 0)
        halves = [pl.ds(r * 1024 + c * 2 + h, B, stride=4) for h in range(2)]

        def put(value):
            for h in range(2):
                out_ref[halves[h], :] = value[:, h * HALF : (h + 1) * HALF]

        def get():
            return jnp.concatenate([mat_ref[halves[h], :] for h in range(2)], axis=1)

        own_first = (j == k) & (i > k)
        own_second = (j == k + 1) & (i > k + 1)
        diagonal = (i == j) & ((j == k) | (j == k + 1))
        plain = jnp.logical_not(own_first | own_second | diagonal)

        @pl.when(plain & (level == 2) & jnp.logical_not(active))
        def _():
            put(get())

        @pl.when(plain & (level == 2) & active)
        def _():
            first = dot_nt(panel[0, row_at], panel[0, col_at])
            put(get() - first - dot_nt(panel[1, row_at], panel[1, col_at]))

        @pl.when(plain & (level == 1) & jnp.logical_not(active))
        def _():
            put(rounded(get()))

        @pl.when(plain & (level == 1) & active)
        def _():
            once = rounded(rounded(get()) - dot_narrow(panel[0, row_at], panel[0, col_at]))
            put(rounded(once - dot_narrow(panel[1, row_at], panel[1, col_at])))

        @pl.when(plain & (level == 0))
        def _():
            put(jnp.zeros((B, B), f32))

        @pl.when(own_first)
        def _():
            put(panel[0, row_at])

        @pl.when(own_second)
        def _():
            put(panel[1, row_at])

        @pl.when(diagonal)
        def _():
            put(f_ref[j - k, 0])

        @pl.when(c == 1)
        def _():
            store(r).start()

        return 0

    lax.fori_loop(0, 8, trail, 0)
    for r in range(4):
        store(r).wait()


def store_to(out_ref, out_hbm, out_sems):
    def store(r):
        at = pl.ds(pl.multiple_of(r * 1024, 1024), 1024)
        return pltpu.make_async_copy(out_ref.at[at], out_hbm.at[at], out_sems.at[r])

    return store


def copies_in(pairs, sems):
    copies = [pltpu.make_async_copy(a, b, sems.at[n]) for n, (a, b) in enumerate(pairs)]
    for copy in copies:
        copy.start()
    return copies


FACTOR_SCRATCH = [
    pltpu.VMEM((N_COL, 6, 8, HALF), f32),
    pltpu.VMEM((2, 2, B, B), f32),
    pltpu.VMEM((B, B), f32),
    pltpu.VMEM((B, B), f32),
    pltpu.VMEM((2, HALF, HALF), f32),
    pltpu.VMEM((2, HALF, HALF), f32),
]


def final_kernel(r0, c0, n_cols, scal, lev, prec, *refs):
    col_hbm, (line_hbm, mat_hbm, out_hbm) = refs[:n_cols], refs[n_cols : n_cols + 3]
    refs = refs[n_cols + 3 :]
    col_refs, (d_ref, rows_ref, mat_ref, out_ref, panel) = refs[:n_cols], refs[n_cols : n_cols + 5]
    d_rows, f_ref, g_ref, s_ref, u_ref, v_ref, sems, out_sems = refs[n_cols + 5 :]
    k, p, q = scal[0], scal[1], scal[2]
    core = p % 2
    rows = 4 - r0
    split = 4 * rows
    pairs = [(line_hbm.at[:, :, split : split + 6], d_ref)]
    pairs += zip(col_hbm, col_refs)
    pairs += [(line_hbm.at[:, :, 0:split], rows_ref), (mat_hbm, mat_ref)]
    fetches = copies_in(pairs, sems)
    fetches[0].wait()
    factor_first(scal, lev, d_ref, d_rows, f_ref, g_ref, s_ref, u_ref, v_ref)
    for fetch in fetches[1:]:
        fetch.wait()
    place_rows(rows, rows_ref, panel)
    for t in range(2):
        for h in range(2):
            lanes = slice(h * HALF, (h + 1) * HALF)
            for c in range(2 - c0):
                for part in range(2):
                    if n_cols == 1:
                        at = slice(part * HALF, (part + 1) * HALF)
                        tile_half = col_refs[0][:, part, t, c, h].reshape(HALF, HALF)
                        panel[t, rows + c, at, lanes] = tile_half
                        continue
                    for y in range(8):
                        at = 8 * (16 * part + 2 * y)
                        for ref, side in zip(col_refs, (core, 1 - core)):
                            to = pl.ds(pl.multiple_of(at + 8 * side, 8), 8)
                            panel[t, rows + c, to, lanes] = ref[y, part, t, c, h]

    def index_of(n):
        if isinstance(n, int):
            return (n + r0) * N_ROW + p if n < rows else (n - rows + c0) * N_COL + q
        return jnp.where(n < rows, (n + r0) * N_ROW + p, (n - rows + c0) * N_COL + q)

    tiles = rows + 2 - c0
    first_panel(tiles, index_of, lev, panel, f_ref, g_ref)
    factor_second(f_ref, s_ref)
    second_panel(tiles, index_of, k, lev, panel, f_ref)
    trail_tiles(
        r0, c0, scal, prec, panel, f_ref, mat_ref, out_ref, store_to(out_ref, out_hbm, out_sems)
    )


def final(r0, c0, scal, lev, prec, cols, line, mat):
    rows = 4 - r0
    return pl.pallas_call(
        functools.partial(final_kernel, r0, c0, len(cols)),
        in_specs=[SMEM, SMEM, SMEM] + [HBM] * (len(cols) + 2),
        out_specs=HBM,
        out_shape=pltpu.HBM(mat.shape, f32),
        scratch_shapes=[
            *[pltpu.VMEM(x.shape, f32) for x in cols],
            pltpu.VMEM((4, 8, 6, 8, HALF), f32),
            pltpu.VMEM((4, 8, 4 * rows, 8, HALF), f32),
            pltpu.VMEM(mat.shape, f32),
            pltpu.VMEM(mat.shape, f32),
            pltpu.VMEM((2, rows + 2 - c0, B, B), f32),
            *FACTOR_SCRATCH,
            pltpu.SemaphoreType.DMA((5,)),
            pltpu.SemaphoreType.DMA((4,)),
        ],
        compiler_params=pltpu.CompilerParams(vmem_limit_bytes=24 << 20),
        cost_estimate=pl.CostEstimate(flops=4 * 10**10, bytes_accessed=10**7, transcendentals=0),
    )(scal, lev, prec, *cols, line, mat)


def cross_pairs(odd):
    pairs = []
    for p in range(N_ROW):
        for q in range(N_COL):
            low = q < N_ROW
            first = low != odd
            row = q if low else q - N_ROW
            col = p if first else p + N_ROW
            pairs.append((p * N_COL + q, row * N_COL + col))
    return pairs


def two_steps(r0, c0, scal, prec, mat):
    both = ("row", "col")
    z_groups = [[4 * z + x for z in range(8)] for x in range(4)]
    x_groups = [[4 * z + x for x in range(4)] for z in range(8)]
    y_groups = [[2 * y + c for y in range(8)] for c in range(2)]

    got_diag = lax.all_to_all(pack_diag(scal, prec, mat), "col", 0, 0)
    seen = lax.all_gather(diag_parts(scal, got_diag), "row")
    got_bulk = lax.all_to_all(pack_bulk(r0, scal, prec, mat), "col", 0, 0)
    lev = seen[:, 4, :, 0].astype(jnp.int32)

    line, even, odd = route(r0, c0, scal, got_bulk, seen)
    line = lax.all_to_all(line, "col", 0, 0, axis_index_groups=z_groups)
    first = lax.ppermute(even, both, cross_pairs(False))
    second = lax.ppermute(odd, both, cross_pairs(True))
    line, first, second, lev = lax.optimization_barrier((line, first, second, lev))

    line = lax.all_to_all(line_copies(line), "col", 0, 0, axis_index_groups=x_groups)
    parts = order_cols(scal, first, second)
    if c0 == 0:
        own = lax.all_gather(parts, "row", axis_index_groups=y_groups)
        other = lax.ppermute(own, "row", [(i, i ^ 1) for i in range(N_ROW)])
        cols = (own, other)
    else:
        cols = (lax.all_gather(parts, "row"),)
    return final(r0, c0, scal, lev, prec, cols, line, mat)


def per_device(matrix, precision, first_col):
    p = lax.axis_index("row")
    q = lax.axis_index("col")
    k = first_col[0]
    scal = jnp.stack([k, p, q]).astype(jnp.int32)
    prec = precision.reshape(4, 2).T
    mat = matrix.reshape(4096, HALF)
    bands = [functools.partial(two_steps, r0, r0 // 2) for r0 in range(3)]
    out = lax.switch(k // N_ROW, bands, scal, prec, mat)
    return out.reshape(matrix.shape)


def solution(mesh):
    in_specs = (P(None, "row", None, None, "col", None), P(None, "row", None, "col"), P())
    out_specs = P(None, "row", None, None, "col", None)
    return jax.shard_map(
        per_device, mesh=mesh, in_specs=in_specs, out_specs=out_specs, check_vma=False
    )
```
